128 devices in a mesh: seq: 8 (over x, y_hi), res: 16 (over y_lo, z, core).
Axes of the slice: x: 4, y: 4 (y_hi: 2, y_lo: 2; y = y_hi * 2 + y_lo), z: 4, core: 2. Of those that a mesh axis runs over, the one named last changes fastest.
Arguments:
- alignment: bfloat16 [256, 512, 256], P('seq', 'res'), may hold values from -6 to 6
- pair_state: bfloat16 [512, 512, 128], P('seq', 'res'), may hold values from -6 to 6
- bias_weight: bfloat16 [128, 8], replicated, may hold values from -15 to 15
- row_weight: bfloat16 [256, 1024], replicated, may hold values from -0.375 to 0.375
- row_output_weight: bfloat16 [256, 256], replicated, may hold values from -0.375 to 0.375
- column_weight: bfloat16 [256, 1024], replicated, may hold values from -2 to 2
- column_output_weight: bfloat16 [256, 256], replicated, may hold values from -0.375 to 0.375
- transition_in: bfloat16 [256, 1024], replicated, may hold values from -0.375 to 0.375
- transition_out: bfloat16 [1024, 256], replicated, may hold values from -0.1875 to 0.1875
- outer_in: bfloat16 [256, 64], replicated, may hold values from -0.375 to 0.375
- outer_out: bfloat16 [1024, 128], replicated, may hold values from -1 to 1
Outputs:
- alignment_out: bfloat16 [256, 512, 256], P(None, ('seq', 'res'))
- pair_update: bfloat16 [512, 512, 128], P('seq', 'res')
The draws below stay inside these ranges and needn't reach their ends.
All inputs are finite; a program needn't handle non-finite values.
Results may differ from the reference program's by a relative error of at most 0.02.
The reference program's roundings to bfloat16 on the way count: a program that leaves them out, or rounds other values in their place, can miss the bound.
Values may be sent and summed in bfloat16 or wider, within the bound.
A program may use at most 128 MiB of HBM per device.

```python
import jax
import jax.numpy as jnp
from jax import lax

C = 256
H = 8
CZ = 128
OC = 32
RES_DEV = 32
S = 256
R = 512


def draw_bias_weight(key, part):
    key = jax.random.fold_in(key, 11)
    normal_draw = jnp.clip(jax.random.normal(key, (CZ, H), jnp.float32), -6.0, 6.0)
    return (normal_draw * 0.09).astype(jnp.bfloat16)


def draw_column_weight(key, part):
    key = jax.random.fold_in(key, 23)
    base = jnp.clip(jax.random.normal(key, (C, 4 * C), jnp.float32), -6.0, 6.0) * 0.0625
    return base.astype(jnp.bfloat16)


def levels(key, dims, split, low, high):
    gain, own = 1.0, jax.random.fold_in(key, 6)
    for axis_at, parts in split:
        heights = jnp.exp(jax.random.uniform(jax.random.fold_in(own, axis_at), (parts,), jnp.float32, low / len(split), high / len(split)))
        gain = gain * jnp.repeat(heights, dims[axis_at] // parts).reshape([-1 if axis == axis_at else 1 for axis in range(len(dims))])
    return gain


def centred(own_key, dims, width, bound, pieces=(), held_as=jnp.bfloat16):
    values = width * jax.random.normal(own_key, dims, jnp.float32)
    if pieces:
        values = values * levels(own_key, dims, pieces, -0.22, 0.18)
    return jnp.clip(values, -bound, bound).astype(held_as)


def setup_inputs(seed: int = 0) -> dict:
    keys = jax.random.split(jax.random.key(seed), 12)
    alignment = centred(keys[0], (S, R, C), 1.0, 6.0, ((0, 8), (1, 16)))
    pair_state = centred(keys[1], (R, R, CZ), 1.0, 6.0, ((0, 8), (1, 16)))
    bias_weight = draw_bias_weight(jax.random.fold_in(keys[11], 71), 0)
    row_weight = centred(keys[3], (C, 4 * C), C ** -0.5, 0.375)
    row_output_weight = centred(keys[4], (C, C), C ** -0.5, 0.375)
    column_weight = draw_column_weight(jax.random.fold_in(keys[11], 71), 0)
    column_output_weight = centred(keys[6], (C, C), C ** -0.5, 0.375)
    transition_in = centred(keys[7], (C, 4 * C), C ** -0.5, 0.375)
    transition_out = centred(keys[8], (4 * C, C), (4 * C) ** -0.5, 0.1875)
    outer_in = centred(keys[9], (C, 2 * OC), C ** -0.5, 0.375)
    outer_out = centred(keys[10], (OC * OC, CZ), OC ** -0.5, 1.0)
    return dict(alignment=alignment, pair_state=pair_state, bias_weight=bias_weight, row_weight=row_weight, row_output_weight=row_output_weight, column_weight=column_weight, column_output_weight=column_output_weight, transition_in=transition_in, transition_out=transition_out, outer_in=outer_in, outer_out=outer_out)


epsilon = 1e-05

def apply_layer_norm(values):
    values = values.astype(jnp.float32)
    center = values - lax.optimization_barrier(jnp.mean(values, axis=-1, keepdims=True))
    spread = lax.optimization_barrier(jnp.mean(center * center, axis=-1, keepdims=True))
    return center / jnp.sqrt(spread + epsilon)

def project_heads(normed_input, weight):
    channels = weight.shape[0]
    head_size = channels // H
    projected = jnp.dot(normed_input, weight, preferred_element_type=jnp.float32)
    queries = (projected[..., :channels] * head_size ** (-0.5)).astype(jnp.bfloat16)
    key_rows = projected[..., channels:2 * channels].astype(jnp.bfloat16)
    value_rows = projected[..., 2 * channels:3 * channels].astype(jnp.bfloat16)
    gating = jax.nn.sigmoid(projected[..., 3 * channels:]).astype(jnp.bfloat16)
    return (queries, key_rows, value_rows, gating)

def attend_one(queries, key_rows, value_rows, bias):
    length, channels = queries.shape
    head_size = channels // H
    query_heads = queries.astype(jnp.float32).reshape(length, H, head_size)
    key_heads = key_rows.astype(jnp.float32).reshape(key_rows.shape[0], H, head_size)
    value_heads = value_rows.astype(jnp.float32).reshape(value_rows.shape[0], H, head_size)
    scores = jnp.einsum('qhd,khd->hqk', query_heads, key_heads, precision=lax.Precision.HIGHEST)
    scores = scores + bias.astype(jnp.float32)
    row_peak = lax.optimization_barrier(jnp.max(scores, axis=-1, keepdims=True))
    exp_terms = jnp.exp(scores - row_peak)
    weights_bf = (exp_terms / lax.optimization_barrier(jnp.sum(exp_terms, axis=-1, keepdims=True))).astype(jnp.bfloat16)
    result = jnp.einsum('hqk,khd->qhd', weights_bf.astype(jnp.float32), value_heads, precision=lax.Precision.HIGHEST)
    return result.reshape(length, channels)

def reference(alignment, pair_state, bias_weight, row_weight, row_output_weight, column_weight, column_output_weight, transition_in, transition_out, outer_in, outer_out):
    pair_norm = apply_layer_norm(pair_state).astype(jnp.bfloat16)
    full_bias = jnp.dot(pair_norm, bias_weight, preferred_element_type=jnp.float32).astype(jnp.bfloat16).transpose(2, 0, 1)
    normed_input = apply_layer_norm(alignment).astype(jnp.bfloat16)
    queries, key_rows, value_rows, gating = project_heads(normed_input, row_weight)

    def one_sequence(inputs):
        return attend_one(inputs[0], inputs[1], inputs[2], full_bias)
    outputs = lax.map(one_sequence, (queries, key_rows, value_rows))
    gated_output_rows = (gating.astype(jnp.float32) * outputs).astype(jnp.bfloat16)
    row_alignment_state = (alignment.astype(jnp.float32) + jnp.dot(gated_output_rows, row_output_weight, preferred_element_type=jnp.float32)).astype(jnp.bfloat16)
    column_normed_input = apply_layer_norm(row_alignment_state).astype(jnp.bfloat16)
    col_queries, col_keys, col_values, col_gating = project_heads(column_normed_input, column_weight)
    zero_bias = jnp.zeros((H, S, S), jnp.float32)

    def one_column(inputs):
        return attend_one(inputs[0], inputs[1], inputs[2], zero_bias)
    col_out = lax.map(one_column, (col_queries.transpose(1, 0, 2), col_keys.transpose(1, 0, 2), col_values.transpose(1, 0, 2))).transpose(1, 0, 2)
    column_gated_result = (col_gating.astype(jnp.float32) * col_out).astype(jnp.bfloat16)
    residual_state = row_alignment_state.astype(jnp.float32) + jnp.dot(column_gated_result, column_output_weight, preferred_element_type=jnp.float32)
    trans_normed = apply_layer_norm(residual_state).astype(jnp.bfloat16)
    hidden = jax.nn.relu(jnp.dot(trans_normed, transition_in, preferred_element_type=jnp.float32)).astype(jnp.bfloat16)
    alignment_out = (residual_state + jnp.dot(hidden, transition_out, preferred_element_type=jnp.float32)).astype(jnp.bfloat16)
    opm_normed = apply_layer_norm(alignment_out).astype(jnp.bfloat16)
    factors = jnp.dot(opm_normed, outer_in, preferred_element_type=jnp.float32).astype(jnp.bfloat16)
    left_side = factors[..., :OC].astype(jnp.float32)
    right_side = factors[..., OC:].astype(jnp.float32)
    left_blocks = left_side.reshape(S, R // RES_DEV, RES_DEV, OC).transpose(1, 0, 2, 3)

    def outer_block(left_block):
        outer_sum = jnp.einsum('sic,sjd->ijcd', left_block, right_side, precision=lax.Precision.HIGHEST) / S
        flattened = outer_sum.astype(jnp.bfloat16).reshape(RES_DEV, R, OC * OC)
        return jnp.dot(flattened, outer_out, preferred_element_type=jnp.float32).astype(jnp.bfloat16)
    pair_update = lax.map(outer_block, left_blocks).reshape(R, R, CZ)
    return (alignment_out, pair_update)
```

```python
import functools

import jax
import jax.numpy as jnp
from jax import lax
from jax.experimental import pallas as pl
from jax.experimental.pallas import tpu as pltpu
from jax.sharding import PartitionSpec as P

H = 8
D = 32
C = 256
SEQ = 8
RES = 16
EPS = 1e-05
MESH = pl.DeviceIdType.MESH
F32 = jnp.float32
BF16 = jnp.bfloat16
ANY = pl.BlockSpec(memory_space=pl.ANY)
VMEM = pl.BlockSpec(memory_space=pltpu.VMEM)
NT = (((1,), (1,)), ((), ()))
TN = (((0,), (0,)), ((), ()))


def layer_norm(values):
    center = values - jnp.mean(values, axis=-1, keepdims=True)
    spread = jnp.mean(center * center, axis=-1, keepdims=True)
    return center * lax.rsqrt(spread + EPS)


def dot(a, b):
    return jnp.dot(a, b, preferred_element_type=F32)


def dot_nt(a, b):
    return lax.dot_general(a, b, NT, preferred_element_type=F32)


def dot_tn(a, b):
    return lax.dot_general(a, b, TN, preferred_element_type=F32)


def bias_kernel(pair_ref, weight_ref, out_ref):
    lane = lax.broadcasted_iota(jnp.int32, (32, 512), 1) % 64
    weight = weight_ref[...]

    def step(k, total):
        rows = pair_ref[pl.ds(k * 8, 8)].reshape(256, 128).astype(F32)
        spread = dot(layer_norm(rows).astype(BF16), weight)
        for one in range(8):
            total = jnp.where(lane == k * 8 + one, spread[one * 32 : one * 32 + 32], total)
        return total

    total = lax.fori_loop(0, 8, step, jnp.zeros((32, 512), F32)).astype(BF16)
    for t in range(4):
        out_ref[t] = total[:, t * 128 : t * 128 + 128]


def pair_bias(pair_state, bias_weight):
    weight = jnp.repeat(bias_weight, 64, axis=1)
    return pl.pallas_call(
        bias_kernel,
        out_shape=jax.ShapeDtypeStruct((4, 32, 128), BF16),
        in_specs=[VMEM, VMEM],
        out_specs=VMEM,
        compiler_params=pltpu.CompilerParams(vmem_limit_bytes=32 << 20),
        name="pair_bias",
    )(pair_state, weight)


def project(x, wt_ref, wk_ref):
    proj = dot_nt(wt_ref[...], x)
    q = (proj[:C] * D ** (-0.5)).astype(BF16)
    v = proj[C : 2 * C].astype(BF16)
    g = jax.nn.sigmoid(proj[2 * C :]).astype(BF16)
    k = dot(x, wk_ref[...]).astype(BF16)
    return q, k, v, g


def row_kernel(x_ref, bias_ref, wt_ref, wk_ref, wo_ref, out_ref, qd, kk, vt, gt, mask, mid, mix):
    row = lax.broadcasted_iota(jnp.int32, (C, 512), 0) // D
    lane = lax.broadcasted_iota(jnp.int32, (C, 512), 1) // 64
    mask[...] = jnp.where(row == lane, 1.0, 0.0).astype(BF16)
    low = lax.broadcasted_iota(jnp.int32, (C, 128), 1) < 64

    for n in range(2):
        x = x_ref[:, n].reshape(512, C).astype(F32)
        q, k, v, g = project(layer_norm(x).astype(BF16), wt_ref, wk_ref)
        kk[n] = k
        vt[n] = v
        for t in range(4):
            gt[n, t] = g[:, t * 128 : t * 128 + 128]
            tile = q[:, t * 128 : t * 128 + 128].astype(F32)
            other = pltpu.roll(tile, 64, axis=1)
            qd[n, 2 * t] = jnp.where(low, tile, other).astype(BF16)
            qd[n, 2 * t + 1] = jnp.where(low, other, tile).astype(BF16)

    low32 = lax.broadcasted_iota(jnp.int32, (D, 128), 1) < 64

    def step(index, carry):
        n = index // 4
        sp = index % 4
        halves = []
        for e in range(2):
            s = sp * 2 + e
            tile = qd[n, s]
            wide = jnp.concatenate([tile] * 4, axis=1) * mask[...]
            bias = jnp.concatenate([bias_ref[t, s] for t in range(4)], axis=1)
            score = dot(kk[n], wide) + bias.astype(F32)
            peak = jnp.max(score, axis=0, keepdims=True)
            terms = jnp.exp(score - peak)
            scale = 1.0 / jnp.sum(terms, axis=0, keepdims=True)
            terms = terms.astype(BF16)
            parts = []
            for half in range(2):
                o = dot(vt[n, half * 128 : half * 128 + 128, :], terms[:, half * 256 : half * 256 + 256])
                o = o * scale[:, half * 256 : half * 256 + 256]
                for h in range(4):
                    part = o[h * D : h * D + D, (h // 2) * 128 : (h // 2) * 128 + 128]
                    if h % 2 != e:
                        part = pltpu.roll(part, 64, axis=1)
                    parts.append(part)
            halves.append(parts)
        ot = jnp.concatenate([jnp.where(low32, a, b) for a, b in zip(*halves)], axis=0)
        gated = (gt[n, sp].astype(F32) * ot).astype(BF16)
        x = x_ref[pl.ds(sp * 4, 4), n].reshape(128, C).astype(F32)
        new = x + dot_tn(gated, wo_ref[...])
        for ch in range(2):
            mid[ch] = new[:, ch * 128 : ch * 128 + 128]
        for ch in range(2):
            for a in range(4):
                mix[pl.ds(sp * 512 + n * 8 + ch * 4 + a, 32, stride=16), :] = mid[ch, pl.ds(a, 32, stride=4), :]
        return carry

    lax.fori_loop(0, 8, step, 0)
    out_ref[...] = mix[...].astype(BF16)


def row_attention(x, bias, wt, wk, wo):
    return pl.pallas_call(
        row_kernel,
        out_shape=jax.ShapeDtypeStruct((2048, 128), BF16),
        in_specs=[VMEM] * 5,
        out_specs=VMEM,
        scratch_shapes=[
            pltpu.VMEM((2, 8, C, 128), BF16),
            pltpu.VMEM((2, 512, C), BF16),
            pltpu.VMEM((2, C, 512), BF16),
            pltpu.VMEM((2, 4, C, 128), BF16),
            pltpu.VMEM((C, 512), BF16),
            pltpu.VMEM((2, 128, 128), F32),
            pltpu.VMEM((2048, 128), F32),
        ],
        compiler_params=pltpu.CompilerParams(vmem_limit_bytes=48 << 20),
        name="row_attention",
    )(x, bias, wt, wk, wo)


def column_kernel(
    x_ref, wt_ref, wk_ref, wo_ref, win_ref, wout_ref, wl_ref, wr_ref,
    out_ref, left_ref, right_ref, mix, ot, right,
):
    mix[...] = x_ref[...].astype(F32)
    head = lax.broadcasted_iota(jnp.int32, (C, C), 0) // D
    right[...] = jnp.zeros_like(right)

    def step(a, carry):
        cells = jnp.concatenate(
            [
                jnp.concatenate([mix[pl.ds(n * 8 + ch * 4 + a, 128, stride=16), :] for ch in range(2)], axis=1)
                for n in range(2)
            ],
            axis=0,
        )
        q, k, v, g = project(layer_norm(cells).astype(BF16), wt_ref, wk_ref)
        for h in range(H):
            one = jnp.where(head == h, q, jnp.zeros_like(q))
            score = dot(k, one)
            peak = jnp.max(score, axis=0, keepdims=True)
            terms = jnp.exp(score - peak)
            scale = 1.0 / jnp.sum(terms, axis=0, keepdims=True)
            ot[h * D : h * D + D, :] = dot(v[h * D : h * D + D], terms.astype(BF16)) * scale
        gated = (g.astype(F32) * ot[...]).astype(BF16)
        stream = cells + dot_tn(gated, wo_ref[...])
        normed = layer_norm(stream).astype(BF16)
        hidden = jnp.maximum(dot(normed, win_ref[...]), 0.0).astype(BF16)
        new = (stream + dot(hidden, wout_ref[...])).astype(BF16).astype(F32)
        for n in range(2):
            for ch in range(2):
                mix[pl.ds(n * 8 + ch * 4 + a, 128, stride=16), :] = new[
                    n * 128 : n * 128 + 128, ch * 128 : ch * 128 + 128
                ]
        factor = layer_norm(new).astype(BF16)
        left_ref[pl.ds(pl.multiple_of(a * D, D), D), :] = dot_nt(wl_ref[...], factor).astype(BF16)
        right[...] += dot(factor, wr_ref[a])
        return carry

    lax.fori_loop(0, 4, step, 0)
    out_ref[...] = mix[...].astype(BF16)
    right_ref[...] = right[...].astype(BF16)


def column_part(x, wt, wk, wo, win, wout, wl, wr):
    return pl.pallas_call(
        column_kernel,
        out_shape=(
            jax.ShapeDtypeStruct((2048, 128), BF16),
            jax.ShapeDtypeStruct((128, 256), BF16),
            jax.ShapeDtypeStruct((256, 128), BF16),
        ),
        in_specs=[VMEM] * 8,
        out_specs=(VMEM, VMEM, VMEM),
        scratch_shapes=[
            pltpu.VMEM((2048, 128), F32),
            pltpu.VMEM((C, 256), F32),
            pltpu.VMEM((256, 128), F32),
        ],
        compiler_params=pltpu.CompilerParams(vmem_limit_bytes=48 << 20),
        name="column_part",
    )(x, wt, wk, wo, win, wout, wl, wr)


def outer_kernel(left_ref, right_ref, w_ref, out_ref, left, wide, block, pairs):
    for n in range(2):
        left[n] = left_ref[:, :, n * 128 : n * 128 + 128].reshape(2048, 128).astype(F32)
    block[...] = jnp.zeros_like(block)
    for c in range(32):
        one = w_ref[c * 32 : c * 32 + 32, :]
        for j in range(4):
            block[c * 128 + j * 32 : c * 128 + j * 32 + 32, j * 128 : j * 128 + 128] = one
    right = jnp.concatenate([right_ref[o] for o in range(8)], axis=1)
    for c in range(0, 32, 2):
        rows = jnp.concatenate(
            [
                jnp.concatenate([left[n, pl.ds(c + k, 64, stride=32), :] for n in range(2)], axis=1)
                for k in range(2)
            ],
            axis=0,
        )
        product = (dot(rows.astype(BF16), right) * (1.0 / 256)).astype(BF16)
        for k in range(2):
            for g in range(8):
                wide[g * 64 : g * 64 + 64, (c + k) * 128 : (c + k) * 128 + 128] = product[
                    k * 64 : k * 64 + 64, g * 128 : g * 128 + 128
                ]
    update = dot(wide[...], block[...])
    for g in range(8):
        for j in range(4):
            pairs[pl.ds(g * 4 + j, 64, stride=32), :] = update[g * 64 : g * 64 + 64, j * 128 : j * 128 + 128]
    out_ref[...] = pairs[...].astype(BF16)


def outer_part(left, right, w):
    return pl.pallas_call(
        outer_kernel,
        out_shape=jax.ShapeDtypeStruct((2048, 128), BF16),
        in_specs=[VMEM] * 3,
        out_specs=VMEM,
        scratch_shapes=[
            pltpu.VMEM((2, 2048, 128), F32),
            pltpu.VMEM((512, 4096), BF16),
            pltpu.VMEM((4096, 512), BF16),
            pltpu.VMEM((2048, 128), F32),
        ],
        compiler_params=pltpu.CompilerParams(vmem_limit_bytes=48 << 20),
        name="outer_part",
    )(left, right, w)


def split_weight(weight):
    q, k, v, g = (weight[:, i * C : i * C + C] for i in range(4))
    return jnp.concatenate([q, v, g], axis=1).T, k


def split_outer(weight):
    left, right = weight[:, :D].T, weight[:, D:]
    return left, jnp.stack([jnp.pad(right, ((0, 0), (a * D, 96 - a * D))) for a in range(4)])


def me():
    return lax.axis_index("seq"), lax.axis_index("res")


def device(x, y, z, core):
    return (x * 2 + y // 2, (y % 2) * 8 + z * 2 + core)


def remote(src, dst, send, recv, target):
    return pltpu.make_async_remote_copy(
        src_ref=src, dst_ref=dst, send_sem=send, recv_sem=recv, device_id=target, device_id_type=MESH
    )


ORDERS = ("zyx", "xzy", "yxz", "zyx")


def gather_kernel(x_ref, own_ref, xo_ref, bo_ref, send, recv, ssend, srecv, xsend, xrecv, lsem):
    s, r = me()
    pos = {"x": s // 2, "y": (s % 2) * 2 + r // 8, "z": (r % 8) // 2}
    core = r % 2

    def near(dim, by):
        at = dict(pos)
        at[dim] = (pos[dim] + by) % 4
        return device(at["x"], at["y"], at["z"], core)

    sibling = (s, r + 1 - 2 * core)
    barrier = pltpu.get_barrier_semaphore()

    def greet(k, carry):
        pl.semaphore_signal(barrier, inc=1, device_id=(s, (r + k) % 16), device_id_type=MESH)
        return carry

    lax.fori_loop(1, 16, greet, 0)
    for dim in "xy":
        for by in (1, 3):
            pl.semaphore_signal(barrier, inc=1, device_id=near(dim, by), device_id_type=MESH)
    pl.semaphore_wait(barrier, 19)

    def box(t, known, dim, at, rows):
        index = [t]
        for d in "xyz":
            index.append(pl.ds(0, 4) if d in known else (at if d == dim else pos[d]))
        return bo_ref.at[(*index, core, rows)]

    everything = pl.ds(0, 32)
    started = []

    def ring(t, phase, k, src, dst, target):
        copy = remote(src, dst, send.at[t, phase, k], recv.at[t, phase, k], target)
        copy.start()
        started.append(copy)
        return copy

    def share(t, k, src, dst):
        copy = remote(src, dst, ssend.at[t, k], srecv, sibling)
        copy.start()
        started.append(copy)

    local = pltpu.make_async_copy(own_ref, bo_ref.at[:, pos["x"], pos["y"], pos["z"], core], lsem.at[0])
    local.start()
    keep = pltpu.make_async_copy(x_ref.at[r], xo_ref.at[r], lsem.at[1])
    keep.start()

    for phase in range(3):
        first = {}
        for t in range(4):
            dim, known = ORDERS[t][phase], ORDERS[t][:phase]
            mine = box(t, known, dim, pos[dim], everything)
            src = own_ref.at[t] if phase == 0 else mine
            for k, by in enumerate((1, 3)):
                first[t, k] = ring(t, phase, k, src, mine, near(dim, by))
            if phase == 0:
                share(t, 0, src, mine)
        if phase == 0:

            def scatter(k, carry):
                to = (r + k) % 16
                remote(x_ref.at[to], xo_ref.at[r], xsend, xrecv, (s, to)).start()
                return carry

            lax.fori_loop(1, 16, scatter, 0)
        second = {}
        for t in range(4):
            dim, known = ORDERS[t][phase], ORDERS[t][:phase]
            for k, by in enumerate((1, 3)):
                first[t, k].wait_recv()
                at = (pos[dim] + (3, 1)[k]) % 4
                rows = pl.ds(16 * k, 16)
                part = box(t, known, dim, at, rows)
                second[t, k] = ring(t, phase, 2 + k, part, part, near(dim, by))
                whole = box(t, known, dim, at, everything)
                share(t, 1 + phase * 4 + k, whole, whole)
        for t in range(4):
            dim, known = ORDERS[t][phase], ORDERS[t][:phase]
            for k in range(2):
                second[t, k].wait_recv()
                part = box(t, known, dim, (pos[dim] + 2) % 4, pl.ds(16 * k, 16))
                share(t, 3 + phase * 4 + k, part, part)
        if phase == 0:
            local.wait()
    keep.wait()
    for copy in started:
        copy.wait_send()
    half = bo_ref.at[:, :, :, :, 0]
    remote(half, half, lsem.at[0], srecv, sibling).wait_recv()
    most = xo_ref.at[pl.ds(0, 15)]
    remote(most, most, xsend, xrecv, sibling).wait()


def gather(x, own):
    return pl.pallas_call(
        gather_kernel,
        out_shape=(
            jax.ShapeDtypeStruct((16, 2, 32, C), BF16),
            jax.ShapeDtypeStruct((4, 4, 4, 4, 2, 32, 128), BF16),
        ),
        in_specs=[ANY, ANY],
        out_specs=(ANY, ANY),
        scratch_shapes=[
            pltpu.SemaphoreType.DMA((4, 3, 4)),
            pltpu.SemaphoreType.DMA((4, 3, 4)),
            pltpu.SemaphoreType.DMA((4, 13)),
            pltpu.SemaphoreType.DMA,
            pltpu.SemaphoreType.DMA,
            pltpu.SemaphoreType.DMA,
            pltpu.SemaphoreType.DMA((2,)),
        ],
        compiler_params=pltpu.CompilerParams(collective_id=0, has_side_effects=True),
        name="gather",
    )(x, own)


def exchange_kernel(x_ref, out_ref, send, recv, lsem):
    s, r = me()
    here = s * RES + r
    barrier = pltpu.get_barrier_semaphore()

    def greet(k, carry):
        to = (here + k) % 128
        pl.semaphore_signal(barrier, inc=1, device_id=(to // RES, to % RES), device_id_type=MESH)
        return carry

    lax.fori_loop(1, 128, greet, 0)
    keep = pltpu.make_async_copy(x_ref.at[here], out_ref.at[here], lsem)
    keep.start()
    pl.semaphore_wait(barrier, 127)

    def scatter(k, carry):
        to = (here + k) % 128
        remote(x_ref.at[to], out_ref.at[here], send, recv, (to // RES, to % RES)).start()
        return carry

    lax.fori_loop(1, 128, scatter, 0)
    keep.wait()
    most = out_ref.at[pl.ds(0, 127)]
    remote(most, most, send, recv, (s, (r + 1) % RES)).wait()


def exchange(x):
    return pl.pallas_call(
        exchange_kernel,
        out_shape=jax.ShapeDtypeStruct((128, 16, 128), BF16),
        in_specs=[ANY],
        out_specs=ANY,
        scratch_shapes=[pltpu.SemaphoreType.DMA] * 3,
        compiler_params=pltpu.CompilerParams(collective_id=1, has_side_effects=True),
        name="exchange",
    )(x.reshape(128, 16, 128)).reshape(2048, 128)


def factors_kernel(left_ref, right_ref, lo_ref, ro_ref, lsend, lrecv, fsend, frecv, rsend, rrecv, own):
    s, r = me()
    core = r % 2
    chip = r // 2
    sibling = (s, r + 1 - 2 * core)
    column = 2 * s + r // 8
    source = r // 2
    barrier = pltpu.get_barrier_semaphore()

    def greet(k, carry):
        pl.semaphore_signal(barrier, inc=1, device_id=(s, (r + k) % 16), device_id_type=MESH)
        return carry

    lax.fori_loop(1, 16, greet, 0)
    is_own = column == r

    def greet_right(o, carry):
        owner = (r % 2) * 8 + o

        @pl.when(jnp.logical_or(source != s, owner != r))
        def _():
            pl.semaphore_signal(barrier, inc=1, device_id=(source, owner), device_id_type=MESH)

        return carry

    lax.fori_loop(0, 8, greet_right, 0)
    pl.semaphore_wait(barrier, 15 + 8 - jnp.where(is_own, 1, 0))

    keep = pltpu.make_async_copy(left_ref, lo_ref.at[r], own)
    keep.start()
    to_sibling = remote(left_ref, lo_ref.at[r], fsend, frecv, sibling)
    to_sibling.start()
    copies = []
    for k in range(1, 8):
        copy = remote(left_ref, lo_ref.at[r], lsend.at[k], lrecv.at[k], (s, ((chip + k) % 8) * 2 + core))
        copy.start()
        copies.append(copy)

    def send_right(k, carry):
        to = (s + k) % 8

        @pl.when(jnp.logical_not(jnp.logical_and(is_own, k == 0)))
        def _():
            remote(right_ref, ro_ref.at[r % 8], rsend, rrecv, (to, column)).start()

        return carry

    lax.fori_loop(0, 8, send_right, 0)
    keep.wait()

    @pl.when(is_own)
    def _():
        mine = pltpu.make_async_copy(right_ref, ro_ref.at[r % 8], own)
        mine.start()
        mine.wait()

    for k in range(1, 8):
        copies[k - 1].wait_recv()
        got = lo_ref.at[((chip + 8 - k) % 8) * 2 + core]
        remote(got, got, fsend, frecv, sibling).start()
    for copy in copies:
        copy.wait_send()
    half = lo_ref.at[pl.ds(0, 8)]
    remote(half, half, fsend, frecv, sibling).wait()

    @pl.when(is_own)
    def _():
        most = ro_ref.at[pl.ds(0, 7)]
        remote(most, most, rsend, rrecv, sibling).wait()

    @pl.when(jnp.logical_not(is_own))
    def _():
        remote(ro_ref, ro_ref, rsend, rrecv, sibling).wait()


def share_factors(left, right):
    return pl.pallas_call(
        factors_kernel,
        out_shape=(
            jax.ShapeDtypeStruct((16, 128, 256), BF16),
            jax.ShapeDtypeStruct((8, 256, 128), BF16),
        ),
        in_specs=[ANY, ANY],
        out_specs=(ANY, ANY),
        scratch_shapes=[
            pltpu.SemaphoreType.DMA((8,)),
            pltpu.SemaphoreType.DMA((8,)),
        ]
        + [pltpu.SemaphoreType.DMA] * 5,
        compiler_params=pltpu.CompilerParams(collective_id=2, has_side_effects=True),
        name="share_factors",
    )(left, right)


def body(
    alignment,
    pair_state,
    bias_weight,
    row_weight,
    row_output_weight,
    column_weight,
    column_output_weight,
    transition_in,
    transition_out,
    outer_in,
    outer_out,
):
    own = pair_bias(pair_state, bias_weight)
    x, bias = gather(alignment.reshape(16, 2, 32, C), own)
    wt, wk = split_weight(row_weight)
    mid = row_attention(x, bias.reshape(4, 8, 512, 128), wt, wk, row_output_weight)
    cells = exchange(mid)
    wt, wk = split_weight(column_weight)
    wl, wr = split_outer(outer_in)
    new, left, right = column_part(
        cells, wt, wk, column_output_weight, transition_in, transition_out, wl, wr
    )
    left, right = share_factors(left, right)
    pair_update = outer_part(left, right, outer_out).reshape(64, 32, 128)
    alignment_out = new.reshape(128, 2, 2, 4, 128).transpose(0, 1, 3, 2, 4).reshape(256, 4, C)
    return (alignment_out, pair_update)


def solution(mesh):
    in_specs = (P("seq", "res", None), P("seq", "res", None)) + (P(),) * 9
    out_specs = (P(None, ("seq", "res"), None), P("seq", "res", None))
    return jax.shard_map(body, mesh=mesh, in_specs=in_specs, out_specs=out_specs, check_vma=False)
```

```python
import functools

import jax
import jax.numpy as jnp
from jax import lax
from jax.experimental import pallas as pl
from jax.experimental.pallas import tpu as pltpu
from jax.sharding import PartitionSpec as P

H = 8
D = 32
C = 256
SEQ = 8
RES = 16
EPS = 1e-05
MESH = pl.DeviceIdType.MESH
F32 = jnp.float32
BF16 = jnp.bfloat16
ANY = pl.BlockSpec(memory_space=pl.ANY)
VMEM = pl.BlockSpec(memory_space=pltpu.VMEM)
NT = (((1,), (1,)), ((), ()))
TN = (((0,), (0,)), ((), ()))


def layer_norm(values):
    center = values - jnp.mean(values, axis=-1, keepdims=True)
    spread = jnp.mean(center * center, axis=-1, keepdims=True)
    return center * lax.rsqrt(spread + EPS)


def dot(a, b):
    return jnp.dot(a, b, preferred_element_type=F32)


def dot_nt(a, b):
    return lax.dot_general(a, b, NT, preferred_element_type=F32)


def dot_tn(a, b):
    return lax.dot_general(a, b, TN, preferred_element_type=F32)


def project(x, wt, wk):
    proj = dot_nt(wt, x)
    q = (proj[:C] * D ** (-0.5)).astype(BF16)
    v = proj[C : 2 * C].astype(BF16)
    g = jax.nn.sigmoid(proj[2 * C :]).astype(BF16)
    k = dot(x, wk).astype(BF16)
    return q, k, v, g


def device(x, y, z, core):
    return (x * 2 + y // 2, (y % 2) * 8 + z * 2 + core)


def remote(src, dst, send, recv, target):
    return pltpu.make_async_remote_copy(
        src_ref=src, dst_ref=dst, send_sem=send, recv_sem=recv, device_id=target, device_id_type=MESH
    )


ORDERS = ("zyx", "xzy", "yxz", "zyx")


def pair_bias(pair_ref, weight_ref, out_ref):
    lane = lax.broadcasted_iota(jnp.int32, (32, 512), 1) % 64
    low = lax.broadcasted_iota(jnp.int32, (128, 128), 1) < 64
    narrow = weight_ref[...].astype(F32)
    weight = jnp.concatenate(
        [jnp.where(low, narrow[:, 2 * t : 2 * t + 1], narrow[:, 2 * t + 1 : 2 * t + 2]) for t in range(4)], axis=1
    ).astype(BF16)

    def step(k, total):
        rows = pair_ref[pl.ds(k * 8, 8)].reshape(256, 128).astype(F32)
        spread = dot(layer_norm(rows).astype(BF16), weight)
        for one in range(8):
            total = jnp.where(lane == k * 8 + one, spread[one * 32 : one * 32 + 32], total)
        return total

    total = lax.fori_loop(0, 8, step, jnp.zeros((32, 512), F32)).astype(BF16)
    for t in range(4):
        out_ref[t] = total[:, t * 128 : t * 128 + 128]


def row_project(n, x_ref, wt, wk, qd, kk, vt, gt):
    low = lax.broadcasted_iota(jnp.int32, (C, 128), 1) < 64
    x = x_ref[:, n].reshape(512, C).astype(F32)
    q, k, v, g = project(layer_norm(x).astype(BF16), wt[...], wk)
    kk[n] = k
    vt[n] = v
    for t in range(4):
        gt[n, t] = g[:, t * 128 : t * 128 + 128]
        tile = q[:, t * 128 : t * 128 + 128].astype(F32)
        other = pltpu.roll(tile, 64, axis=1)
        qd[n, 2 * t] = jnp.where(low, tile, other).astype(BF16)
        qd[n, 2 * t + 1] = jnp.where(low, other, tile).astype(BF16)


def row_attend(n, sp, x_ref, bias_ref, wo, qd, kk, vt, gt, mask, mid, mix):
    low = lax.broadcasted_iota(jnp.int32, (D, 128), 1) < 64
    halves = []
    for e in range(2):
        tile = qd[n, sp * 2 + e]
        wide = jnp.concatenate([tile] * 4, axis=1) * mask[...]
        bias = jnp.concatenate([bias_ref[t, sp, 2 * e : 2 * e + 2].reshape(512, 128) for t in range(4)], axis=1)
        score = dot(kk[n], wide) + bias.astype(F32)
        peak = jnp.max(score, axis=0, keepdims=True)
        terms = jnp.exp(score - peak)
        scale = 1.0 / jnp.sum(terms, axis=0, keepdims=True)
        terms = terms.astype(BF16)
        parts = []
        for half in range(2):
            o = dot(vt[n, half * 128 : half * 128 + 128, :], terms[:, half * 256 : half * 256 + 256])
            o = o * scale[:, half * 256 : half * 256 + 256]
            for h in range(4):
                part = o[h * D : h * D + D, (h // 2) * 128 : (h // 2) * 128 + 128]
                if h % 2 != e:
                    part = pltpu.roll(part, 64, axis=1)
                parts.append(part)
        halves.append(parts)
    ot = jnp.concatenate([jnp.where(low, a, b) for a, b in zip(*halves)], axis=0)
    gated = (gt[n, sp].astype(F32) * ot).astype(BF16)
    x = x_ref[pl.ds(sp * 4, 4), n].reshape(128, C).astype(F32)
    new = x + dot_tn(gated, wo[...])
    for ch in range(2):
        mid[ch] = new[:, ch * 128 : ch * 128 + 128]
    for ch in range(2):
        for a in range(4):
            mix[pl.ds(sp * 512 + n * 8 + ch * 4 + a, 32, stride=16), :] = mid[ch, pl.ds(a, 32, stride=4), :]


def column_step(a, mix, wt, wk, wo, win, wout, wf, ot):
    head = lax.broadcasted_iota(jnp.int32, (C, C), 0) // D
    cells = jnp.concatenate(
        [
            jnp.concatenate([mix[pl.ds(n * 8 + ch * 4 + a, 128, stride=16), :] for ch in range(2)], axis=1)
            for n in range(2)
        ],
        axis=0,
    )
    q, k, v, g = project(layer_norm(cells).astype(BF16), wt[...], wk)
    for h in range(H):
        one = jnp.where(head == h, q, jnp.zeros_like(q))
        score = dot(k, one)
        peak = jnp.max(score, axis=0, keepdims=True)
        terms = jnp.exp(score - peak)
        scale = 1.0 / jnp.sum(terms, axis=0, keepdims=True)
        ot[h * D : h * D + D, :] = dot(v[h * D : h * D + D], terms.astype(BF16)) * scale
    gated = (g.astype(F32) * ot[...]).astype(BF16)
    stream = cells + dot_tn(gated, wo[...])
    normed = layer_norm(stream).astype(BF16)
    hidden = jnp.maximum(dot(normed, win[...]), 0.0).astype(BF16)
    new = (stream + dot(hidden, wout[...])).astype(BF16).astype(F32)
    for n in range(2):
        for ch in range(2):
            mix[pl.ds(n * 8 + ch * 4 + a, 128, stride=16), :] = new[
                n * 128 : n * 128 + 128, ch * 128 : ch * 128 + 128
            ]
    return dot_nt(wf[...], layer_norm(new).astype(BF16)).astype(BF16)


def outer_weight(w_ref, block):
    block[...] = jnp.zeros_like(block)
    for c in range(32):
        one = w_ref[c * 32 : c * 32 + 32, :]
        for j in range(4):
            block[c * 128 + j * 32 : c * 128 + j * 32 + 32, j * 128 : j * 128 + 128] = one


def outer_part(left_ref, right_ref, out_ref, left, wide, block, pairs):
    for n in range(2):
        left[n] = left_ref[:, :, :, n * 128 : n * 128 + 128].reshape(2048, 128).astype(F32)
    right = right_ref[...].reshape(1024, 256)
    for c in range(0, 32, 2):
        rows = jnp.concatenate(
            [
                jnp.concatenate([left[n, pl.ds(c + k, 64, stride=32), :] for n in range(2)], axis=1)
                for k in range(2)
            ],
            axis=0,
        )
        product = (dot_nt(rows.astype(BF16), right) * (1.0 / 256)).astype(BF16)
        for k in range(2):
            for g in range(8):
                wide[g * 64 : g * 64 + 64, (c + k) * 128 : (c + k) * 128 + 128] = product[
                    k * 64 : k * 64 + 64, g * 128 : g * 128 + 128
                ]
    update = dot(wide[...], block[...])
    for g in range(8):
        for j in range(4):
            pairs[pl.ds(g * 4 + j, 64, stride=32), :] = update[g * 64 : g * 64 + 64, j * 128 : j * 128 + 128]
    out_ref[...] = pairs[...].astype(BF16)


def whole_kernel(
    x_hbm, pair_hbm, bw_hbm, rw_hbm, ro_hbm, cw_hbm, co_hbm, ti_hbm, to_hbm, oi_hbm, oo_hbm,
    ao_hbm, pu_hbm,
    pair, bw, rw, ro, cw, co, ti, to, oi, oo,
    own, xo, bias, qd, kk, vt, gt, mask, mid, mix, wt, sendbuf, cells, ot, fl, fr, lo, ri, left, wide, block, pairs,
    ao, pu,
    send, recv, ssend, srecv, xsend, xrecv, csend, crecv, lsend, lrecv, rsend, rrecv, lsem,
):
    s, r = lax.axis_index("seq"), lax.axis_index("res")
    here = s * RES + r
    pos = {"x": s // 2, "y": (s % 2) * 2 + r // 8, "z": (r % 8) // 2}
    core = r % 2
    sibling = (s, r + 1 - 2 * core)

    def near(dim, by):
        at = dict(pos)
        at[dim] = (pos[dim] + by) % 4
        return device(at["x"], at["y"], at["z"], core)

    loads = {}
    for k, (name, src, dst) in enumerate(
        (
            ("pair", pair_hbm, pair), ("bw", bw_hbm, bw), ("rw", rw_hbm, rw), ("ro", ro_hbm, ro), ("cw", cw_hbm, cw),
            ("co", co_hbm, co), ("ti", ti_hbm, ti), ("to", to_hbm, to), ("oi", oi_hbm, oi), ("oo", oo_hbm, oo),
            ("keep", x_hbm.at[r], xo.at[r]),
        )
    ):
        loads[name] = pltpu.make_async_copy(src, dst, lsem.at[k])
        loads[name].start()
    barrier = pltpu.get_barrier_semaphore()

    def greet(k, carry):
        other = (here + k) % 128
        pl.semaphore_signal(barrier, inc=1, device_id=(other // RES, other % RES), device_id_type=MESH)
        return carry

    lax.fori_loop(1, 128, greet, 0)

    loads["pair"].wait()
    loads["bw"].wait()
    pair_bias(pair, bw, own)
    mine_at = bias.at[:, pos["x"], pos["y"], pos["z"], core]
    place = pltpu.make_async_copy(own, mine_at, lsem.at[0])
    place.start()
    pl.semaphore_wait(barrier, 127)

    def box(t, known, dim, at, rows):
        index = [t]
        for d in "xyz":
            index.append(pl.ds(0, 4) if d in known else (at if d == dim else pos[d]))
        return bias.at[(*index, core, rows)]

    everything = pl.ds(0, 32)
    started = []

    def ring(t, phase, k, src, dst, target):
        copy = remote(src, dst, send.at[t, phase, k], recv.at[t, phase, k], target)
        copy.start()
        started.append(copy)
        return copy

    def share(t, k, src, dst):
        copy = remote(src, dst, ssend.at[t, k], srecv, sibling)
        copy.start()
        started.append(copy)

    def between(phase, half):
        if phase == 0 and half == 0:
            row = lax.broadcasted_iota(jnp.int32, (C, 512), 0) // D
            lane = lax.broadcasted_iota(jnp.int32, (C, 512), 1) // 64
            mask[...] = jnp.where(row == lane, 1.0, 0.0).astype(BF16)
            loads["rw"].wait()
            loads["cw"].wait()
            for k, w in enumerate((rw, cw)):
                for i, at in enumerate((0, 2, 3)):
                    wt[k, i * C : i * C + C, :] = w[:, at * C : at * C + C].T
        if phase == 0 and half == 1:
            loads["oo"].wait()
            outer_weight(oo, block)
        if phase == 1 and half == 1:
            loads["keep"].wait()
            most = xo.at[pl.ds(0, 15)]
            remote(most, most, xsend, xrecv, sibling).wait()
        if phase == 2:
            row_project(half, xo, wt.at[0], rw[:, C : 2 * C], qd, kk, vt, gt)

    for phase in range(3):
        first = {}
        for t in range(4):
            dim, known = ORDERS[t][phase], ORDERS[t][:phase]
            mine = box(t, known, dim, pos[dim], everything)
            src = own.at[t] if phase == 0 else mine
            for k, by in enumerate((1, 3)):
                first[t, k] = ring(t, phase, k, src, mine, near(dim, by))
            if phase == 0:
                share(t, 0, src, mine)
        if phase == 0:

            def scatter(k, carry):
                other = (r + k) % 16
                remote(x_hbm.at[other], xo.at[r], xsend, xrecv, (s, other)).start()
                return carry

            lax.fori_loop(1, 16, scatter, 0)
        between(phase, 0)
        second = {}
        for t in range(4):
            dim, known = ORDERS[t][phase], ORDERS[t][:phase]
            for k, by in enumerate((1, 3)):
                first[t, k].wait_recv()
                at = (pos[dim] + (3, 1)[k]) % 4
                part = box(t, known, dim, at, pl.ds(16 * k, 16))
                second[t, k] = ring(t, phase, 2 + k, part, part, near(dim, by))
                all_of = box(t, known, dim, at, everything)
                share(t, 1 + phase * 4 + k, all_of, all_of)
        between(phase, 1)
        for t in range(4):
            dim, known = ORDERS[t][phase], ORDERS[t][:phase]
            for k in range(2):
                second[t, k].wait_recv()
                part = box(t, known, dim, (pos[dim] + 2) % 4, pl.ds(16 * k, 16))
                share(t, 3 + phase * 4 + k, part, part)
        if phase == 0:
            place.wait()
    half = bias.at[:, :, :, :, 0]
    remote(half, half, lsem.at[0], srecv, sibling).wait_recv()

    loads["ro"].wait()

    def quarter(k, carry):
        sp = (pos["x"] + k) % 4

        def one(n, carry):
            row_attend(n, sp, xo, bias, ro, qd, kk, vt, gt, mask, mid, mix)
            return carry

        lax.fori_loop(0, 2, one, 0)
        rows = mix[pl.ds(pl.multiple_of(sp * 512, 512), 512), :].astype(BF16)
        sendbuf[pl.ds(sp * 32, 32)] = rows.reshape(32, 16, 128)

        def scatter(i, carry):
            other = sp * 32 + (here + i) % 32

            @pl.when(other != here)
            def _():
                remote(sendbuf.at[other], cells.at[here], csend, crecv, (other // RES, other % RES)).start()

            return carry

        lax.fori_loop(0, 32, scatter, 0)
        return carry

    lax.fori_loop(0, 4, quarter, 0)
    cells[here] = sendbuf[here]
    for copy in started:
        copy.wait_send()
    for name in ("cw", "co", "ti", "to", "oi"):
        if name != "cw":
            loads[name].wait()
    most = cells.at[pl.ds(0, 127)]
    remote(most, most, csend, crecv, sibling).wait()

    mix[...] = cells[...].reshape(2048, 128).astype(F32)
    wf = oi[...].T
    column = 2 * s + r // 8
    is_own = column == r

    def residue(a, carry):
        factor = column_step(a, mix, wt.at[1], cw[:, C : 2 * C], co, ti, to, wf, ot)
        fl[a] = factor[:D]
        fr[a] = factor[D:]
        lo[r, a] = factor[:D]

        @pl.when(is_own)
        def _():
            ri[r % 8, a] = factor[D:]

        def send_left(k, carry):
            remote(fl.at[a], lo.at[r, a], lsend, lrecv, (s, (r + k) % 16)).start()
            return carry

        def send_right(k, carry):
            @pl.when(jnp.logical_not(jnp.logical_and(is_own, k == 0)))
            def _():
                remote(fr.at[a], ri.at[r % 8, a], rsend, rrecv, ((s + k) % 8, column)).start()

            return carry

        lax.fori_loop(1, 16, send_left, 0)
        lax.fori_loop(0, 8, send_right, 0)
        return carry

    lax.fori_loop(0, 4, residue, 0)
    ao[...] = mix[...].astype(BF16)
    save = pltpu.make_async_copy(ao, ao_hbm, lsem.at[0])
    save.start()
    most = lo.at[pl.ds(0, 15)]
    remote(most, most, lsend, lrecv, sibling).wait()

    @pl.when(is_own)
    def _():
        part = ri.at[pl.ds(0, 7)]
        remote(part, part, rsend, rrecv, sibling).wait()

    @pl.when(jnp.logical_not(is_own))
    def _():
        remote(ri, ri, rsend, rrecv, sibling).wait()

    outer_part(lo, ri, pu, left, wide, block, pairs)
    last = pltpu.make_async_copy(pu, pu_hbm, lsem.at[1])
    last.start()
    last.wait()
    save.wait()


def body(
    alignment,
    pair_state,
    bias_weight,
    row_weight,
    row_output_weight,
    column_weight,
    column_output_weight,
    transition_in,
    transition_out,
    outer_in,
    outer_out,
):
    dma = pltpu.SemaphoreType.DMA
    new, update = pl.pallas_call(
        whole_kernel,
        out_shape=(jax.ShapeDtypeStruct((2048, 128), BF16), jax.ShapeDtypeStruct((2048, 128), BF16)),
        in_specs=[ANY] * 11,
        out_specs=(ANY, ANY),
        scratch_shapes=[
            pltpu.VMEM((64, 32, 128), BF16),
            pltpu.VMEM((128, 8), BF16),
            pltpu.VMEM((C, 4 * C), BF16),
            pltpu.VMEM((C, C), BF16),
            pltpu.VMEM((C, 4 * C), BF16),
            pltpu.VMEM((C, C), BF16),
            pltpu.VMEM((C, 4 * C), BF16),
            pltpu.VMEM((4 * C, C), BF16),
            pltpu.VMEM((C, 64), BF16),
            pltpu.VMEM((1024, 128), BF16),
            pltpu.VMEM((4, 32, 128), BF16),
            pltpu.VMEM((16, 2, 32, C), BF16),
            pltpu.VMEM((4, 4, 4, 4, 2, 32, 128), BF16),
            pltpu.VMEM((2, 8, C, 128), BF16),
            pltpu.VMEM((2, 512, C), BF16),
            pltpu.VMEM((2, C, 512), BF16),
            pltpu.VMEM((2, 4, C, 128), BF16),
            pltpu.VMEM((C, 512), BF16),
            pltpu.VMEM((2, 128, 128), F32),
            pltpu.VMEM((2048, 128), F32),
            pltpu.VMEM((2, 3 * C, C), BF16),
            pltpu.VMEM((128, 16, 128), BF16),
            pltpu.VMEM((128, 16, 128), BF16),
            pltpu.VMEM((C, 256), F32),
            pltpu.VMEM((4, D, 256), BF16),
            pltpu.VMEM((4, D, 256), BF16),
            pltpu.VMEM((16, 4, D, 256), BF16),
            pltpu.VMEM((8, 4, D, 256), BF16),
            pltpu.VMEM((2, 2048, 128), F32),
            pltpu.VMEM((512, 4096), BF16),
            pltpu.VMEM((4096, 512), BF16),
            pltpu.VMEM((2048, 128), F32),
            pltpu.VMEM((2048, 128), BF16),
            pltpu.VMEM((2048, 128), BF16),
            dma((4, 3, 4)),
            dma((4, 3, 4)),
            dma((4, 13)),
        ]
        + [dma] * 9
        + [dma((11,))],
        compiler_params=pltpu.CompilerParams(collective_id=0, has_side_effects=True, vmem_limit_bytes=56 << 20),
        name="evoformer",
    )(
        alignment.reshape(16, 2, 32, C),
        pair_state,
        bias_weight,
        row_weight,
        row_output_weight,
        column_weight,
        column_output_weight,
        transition_in,
        transition_out,
        outer_in,
        outer_out,
    )
    pair_update = update.reshape(64, 32, 128)
    alignment_out = new.reshape(128, 2, 2, 4, 128).transpose(0, 1, 3, 2, 4).reshape(256, 4, C)
    return (alignment_out, pair_update)


def solution(mesh):
    in_specs = (P("seq", "res", None), P("seq", "res", None)) + (P(),) * 9
    out_specs = (P(None, ("seq", "res"), None), P("seq", "res", None))
    return jax.shard_map(body, mesh=mesh, in_specs=in_specs, out_specs=out_specs, check_vma=False)
```

```python
import functools

import jax
import jax.numpy as jnp
from jax import lax
from jax.experimental import pallas as pl
from jax.experimental.pallas import tpu as pltpu
from jax.sharding import PartitionSpec as P

H = 8
D = 32
C = 256
SEQ = 8
RES = 16
EPS = 1e-05
MESH = pl.DeviceIdType.MESH
F32 = jnp.float32
BF16 = jnp.bfloat16
ANY = pl.BlockSpec(memory_space=pl.ANY)
VMEM = pl.BlockSpec(memory_space=pltpu.VMEM)
NT = (((1,), (1,)), ((), ()))
TN = (((0,), (0,)), ((), ()))


def layer_norm(values):
    center = values - jnp.mean(values, axis=-1, keepdims=True)
    spread = jnp.mean(center * center, axis=-1, keepdims=True)
    return center * lax.rsqrt(spread + EPS)


def dot(a, b):
    return jnp.dot(a, b, preferred_element_type=F32)


def dot_nt(a, b):
    return lax.dot_general(a, b, NT, preferred_element_type=F32)


def dot_tn(a, b):
    return lax.dot_general(a, b, TN, preferred_element_type=F32)


def project(x, wt, wk):
    proj = dot_nt(wt, x)
    q = (proj[:C] * D ** (-0.5)).astype(BF16)
    v = proj[C : 2 * C].astype(BF16)
    g = jax.nn.sigmoid(proj[2 * C :]).astype(BF16)
    k = dot(x, wk).astype(BF16)
    return q, k, v, g


def device(x, y, z, core):
    return (x * 2 + y // 2, (y % 2) * 8 + z * 2 + core)


def remote(src, dst, send, recv, target):
    return pltpu.make_async_remote_copy(
        src_ref=src, dst_ref=dst, send_sem=send, recv_sem=recv, device_id=target, device_id_type=MESH
    )


def pair_bias(pair_ref, weight_ref, out_ref):
    lane = lax.broadcasted_iota(jnp.int32, (32, 512), 1) % 64
    narrow = weight_ref[...].astype(F32)
    weight = jnp.concatenate([jnp.broadcast_to(narrow[h : h + 1], (64, 128)) for h in range(8)], axis=0).astype(BF16)

    def step(k, total):
        rows = pair_ref[pl.ds(k * 8, 8)].reshape(256, 128).astype(F32)
        spread = dot_nt(layer_norm(rows).astype(BF16), weight)
        for one in range(8):
            total = jnp.where(lane == k * 8 + one, spread[one * 32 : one * 32 + 32], total)
        return total

    total = lax.fori_loop(0, 8, step, jnp.zeros((32, 512), F32)).astype(BF16)
    for t in range(4):
        out_ref[t] = total[:, t * 128 : t * 128 + 128]


def row_project(n, x_ref, wt, wk, qd, kk, vt, gt):
    low = lax.broadcasted_iota(jnp.int32, (C, 128), 1) < 64
    x = x_ref[:, n].reshape(512, C).astype(F32)
    q, k, v, g = project(layer_norm(x).astype(BF16), wt[...], wk)
    kk[n] = k
    vt[n] = v
    for t in range(4):
        gt[n, t] = g[:, t * 128 : t * 128 + 128]
        tile = q[:, t * 128 : t * 128 + 128].astype(F32)
        other = pltpu.roll(tile, 64, axis=1)
        qd[n, 2 * t] = jnp.where(low, tile, other).astype(BF16)
        qd[n, 2 * t + 1] = jnp.where(low, other, tile).astype(BF16)


def row_attend(n, sp, x_ref, bias_ref, wo, qd, kk, vt, gt, mask, mid, mix):
    low = lax.broadcasted_iota(jnp.int32, (D, 128), 1) < 64
    halves = []
    for e in range(2):
        tile = qd[n, sp * 2 + e]
        wide = jnp.concatenate([tile] * 4, axis=1) * mask[...]
        bias = jnp.concatenate([bias_ref[t, sp, 2 * e : 2 * e + 2].reshape(512, 128) for t in range(4)], axis=1)
        score = dot(kk[n], wide) + bias.astype(F32)
        peak = jnp.max(score, axis=0, keepdims=True)
        terms = jnp.exp(score - peak)
        scale = 1.0 / jnp.sum(terms, axis=0, keepdims=True)
        terms = terms.astype(BF16)
        parts = []
        for half in range(2):
            o = dot(vt[n, half * 128 : half * 128 + 128, :], terms[:, half * 256 : half * 256 + 256])
            o = o * scale[:, half * 256 : half * 256 + 256]
            for h in range(4):
                part = o[h * D : h * D + D, (h // 2) * 128 : (h // 2) * 128 + 128]
                if h % 2 != e:
                    part = pltpu.roll(part, 64, axis=1)
                parts.append(part)
        halves.append(parts)
    ot = jnp.concatenate([jnp.where(low, a, b) for a, b in zip(*halves)], axis=0)
    gated = (gt[n, sp].astype(F32) * ot).astype(BF16)
    x = x_ref[pl.ds(sp * 4, 4), n].reshape(128, C).astype(F32)
    new = x + dot_tn(gated, wo[...])
    for ch in range(2):
        mid[ch] = new[:, ch * 128 : ch * 128 + 128]
    for ch in range(2):
        for a in range(4):
            mix[pl.ds(sp * 512 + n * 8 + ch * 4 + a, 32, stride=16), :] = mid[ch, pl.ds(a, 32, stride=4), :]


def column_step(a, mix, wt, wk, wo, win, wout, wf, ot):
    head = lax.broadcasted_iota(jnp.int32, (C, C), 0) // D
    cells = jnp.concatenate(
        [
            jnp.concatenate([mix[pl.ds(n * 8 + ch * 4 + a, 128, stride=16), :] for ch in range(2)], axis=1)
            for n in range(2)
        ],
        axis=0,
    )
    q, k, v, g = project(layer_norm(cells).astype(BF16), wt[...], wk)
    for h in range(H):
        one = jnp.where(head == h, q, jnp.zeros_like(q))
        score = dot(k, one)
        peak = jnp.max(score, axis=0, keepdims=True)
        terms = jnp.exp(score - peak)
        scale = 1.0 / jnp.sum(terms, axis=0, keepdims=True)
        ot[h * D : h * D + D, :] = dot(v[h * D : h * D + D], terms.astype(BF16)) * scale
    gated = (g.astype(F32) * ot[...]).astype(BF16)
    stream = cells + dot_tn(gated, wo[...])
    normed = layer_norm(stream).astype(BF16)
    hidden = jnp.maximum(dot(normed, win[...]), 0.0).astype(BF16)
    new = (stream + dot(hidden, wout[...])).astype(BF16).astype(F32)
    for n in range(2):
        for ch in range(2):
            mix[pl.ds(n * 8 + ch * 4 + a, 128, stride=16), :] = new[
                n * 128 : n * 128 + 128, ch * 128 : ch * 128 + 128
            ]
    return dot_nt(wf, layer_norm(new).astype(BF16)).astype(BF16)


def outer_weight(w_ref, block):
    block[...] = jnp.zeros_like(block)
    for c in range(32):
        one = w_ref[c * 32 : c * 32 + 32, :]
        for j in range(4):
            block[c * 128 + j * 32 : c * 128 + j * 32 + 32, j * 128 : j * 128 + 128] = one


def outer_part(left_ref, right_ref, out_ref, left, wide, block, pairs):
    for n in range(2):
        left[n] = left_ref[:, :, :, :, n * 128 : n * 128 + 128].reshape(2048, 128).astype(F32)
    right = right_ref[...].reshape(1024, 256)
    for c in range(0, 32, 2):
        rows = jnp.concatenate(
            [
                jnp.concatenate([left[n, pl.ds(c + k, 64, stride=32), :] for n in range(2)], axis=1)
                for k in range(2)
            ],
            axis=0,
        )
        product = (dot_nt(rows.astype(BF16), right) * (1.0 / 256)).astype(BF16)
        for k in range(2):
            for g in range(8):
                wide[g * 64 : g * 64 + 64, (c + k) * 128 : (c + k) * 128 + 128] = product[
                    k * 64 : k * 64 + 64, g * 128 : g * 128 + 128
                ]
    update = dot(wide[...], block[...])
    for g in range(8):
        for j in range(4):
            pairs[pl.ds(g * 4 + j, 64, stride=32), :] = update[g * 64 : g * 64 + 64, j * 128 : j * 128 + 128]
    out_ref[...] = pairs[...].astype(BF16)


def whole_kernel(
    x_hbm, pair_hbm, bw_hbm, rw_hbm, ro_hbm, cw_hbm, co_hbm, ti_hbm, to_hbm, oi_hbm, oo_hbm,
    ao_hbm, pu_hbm,
    pair, bw, rw, ro, cw, co, ti, to, oi, oo,
    own, xo, bias, qd, kk, vt, gt, mask, mid, mix, wt, sendbuf, cells, ot, fl, fr, lo, ri, left, wide, block, pairs,
    ao, pu,
    zsend, zrecv, ysend, yrecv, hrecv, srecv, lrecv, lsem,
    hsend, ssend, xsend, xrecv, csend, crecv, lsend, fsend, frecv, rsend, rrecv,
):
    s, r = lax.axis_index("seq"), lax.axis_index("res")
    here = s * RES + r
    pos = {"x": s // 2, "y": (s % 2) * 2 + r // 8, "z": (r % 8) // 2}
    core = r % 2
    sibling = (s, r + 1 - 2 * core)

    def near(dim, by):
        at = dict(pos)
        at[dim] = (pos[dim] + by) % 4
        return device(at["x"], at["y"], at["z"], core)

    loads = {}
    for k, (name, src, dst) in enumerate(
        (
            ("pair", pair_hbm, pair), ("bw", bw_hbm, bw), ("rw", rw_hbm, rw), ("ro", ro_hbm, ro), ("cw", cw_hbm, cw),
            ("co", co_hbm, co), ("ti", ti_hbm, ti), ("to", to_hbm, to), ("oi", oi_hbm, oi), ("oo", oo_hbm, oo),
            ("keep", x_hbm.at[r], xo.at[r]),
        )
    ):
        loads[name] = pltpu.make_async_copy(src, dst, lsem.at[k])
        loads[name].start()

    def need(name):
        loads.pop(name).wait()

    barrier = pltpu.get_barrier_semaphore()

    def greet(k, carry):
        other = (here + k) % 128
        pl.semaphore_signal(barrier, inc=1, device_id=(other // RES, other % RES), device_id_type=MESH)
        return carry

    lax.fori_loop(1, 128, greet, 0)

    need("pair")
    need("bw")
    pair_bias(pair, bw, own)
    mine_at = bias.at[:, pos["x"], pos["y"], pos["z"], core]
    place = pltpu.make_async_copy(own, mine_at, lsem.at[0])
    place.start()
    pl.semaphore_wait(barrier, 127)

    def scatter_x(k, carry):
        other = (r + k) % 16
        remote(x_hbm.at[other], xo.at[r], xsend, xrecv, (s, other)).start()
        return carry

    def line(x, y, ts=pl.ds(0, 4)):
        return bias.at[ts, x, y, :, core]

    def share(plane, what):
        remote(what, what, ssend, srecv.at[plane], sibling).start()

    parts = (pl.ds(0, 2), pl.ds(2, 2))
    px, py, pz = pos["x"], pos["y"], pos["z"]

    def along_x(k, y):
        for way, by in enumerate((1, 3)):
            remote(line(px, y), line(px, y), hsend, hrecv.at[k, way], near("x", by)).start()

    def onward_x(k, y):
        for way, by in enumerate((1, 3)):
            x = (px + (3, 1)[way]) % 4
            remote(line(x, y), line(x, y), hsend, hrecv.at[k, way], near("x", by)).wait_recv()
            part = line(x, y, parts[way])
            remote(part, part, hsend, hrecv.at[k, 2 + way], near("x", by)).start()
            share(1 + way, line(x, y))

    def last_x(k, y):
        for way, by in enumerate((1, 3)):
            part = line((px + 2) % 4, y, parts[way])
            remote(part, part, hsend, hrecv.at[k, 2 + way], near("x", by)).wait_recv()
        share(3, line((px + 2) % 4, y))

    def shared(plane, x):
        half = bias.at[:, x, :, :, 1 - core]
        remote(half, half, hsend, srecv.at[plane], sibling).wait_recv()

    first_z = [
        remote(own, bias.at[:, px, py, pz, core], zsend.at[k], zrecv.at[k], near("z", by)) for k, by in enumerate((1, 3, 2))
    ]
    for copy in first_z:
        copy.start()
    lax.fori_loop(1, 16, scatter_x, 0)

    row = lax.broadcasted_iota(jnp.int32, (C, 512), 0) // D
    lane = lax.broadcasted_iota(jnp.int32, (C, 512), 1) // 64
    mask[...] = jnp.where(row == lane, 1.0, 0.0).astype(BF16)
    need("rw")
    for i, at in enumerate((0, 2, 3)):
        wt[0, i * C : i * C + C, :] = rw[:, at * C : at * C + C].T

    place.wait()
    for copy in first_z:
        copy.wait_recv()
    first_y = [
        remote(line(px, py), line(px, py), ysend.at[k], yrecv.at[k], near("y", by)) for k, by in enumerate((1, 3))
    ]
    for copy in first_y:
        copy.start()
    along_x(0, py)
    share(0, line(px, py))
    need("cw")
    for i, at in enumerate((0, 2, 3)):
        wt[1, i * C : i * C + C, :] = cw[:, at * C : at * C + C].T
    second_y = []
    for k, by in enumerate((1, 3)):
        first_y[k].wait_recv()
        y = (py + (3, 1)[k]) % 4
        part = line(px, y, parts[k])
        second_y.append(remote(part, part, ysend.at[2 + k], yrecv.at[2 + k], near("y", by)))
        second_y[k].start()
        along_x(1 + k, y)
        share(0, line(px, y))
    need("oo")
    outer_weight(oo, block)
    for copy in second_y:
        copy.wait_recv()
    along_x(3, (py + 2) % 4)
    share(0, line(px, (py + 2) % 4))
    need("keep")
    most = xo.at[pl.ds(0, 15)]
    remote(most, most, xsend, xrecv, sibling).wait()
    row_project(0, xo, wt.at[0], rw[:, C : 2 * C], qd, kk, vt, gt)
    onward_x(0, py)
    row_project(1, xo, wt.at[0], rw[:, C : 2 * C], qd, kk, vt, gt)
    onward_x(1, (py + 3) % 4)
    need("ro")

    def attend(index, carry):
        q = index // 2
        n = index % 2
        sp = (px + q - q // 2 + 2 * (q % 2) * (1 - q // 2)) % 4

        @pl.when(index == 0)
        def _():
            shared(0, px)

        @pl.when(index == 1)
        def _():
            onward_x(2, (py + 1) % 4)

        @pl.when(index == 2)
        def _():
            onward_x(3, (py + 2) % 4)
            shared(1, (px + 3) % 4)

        @pl.when(index == 3)
        def _():
            last_x(0, py)

        @pl.when(index == 4)
        def _():
            shared(2, (px + 1) % 4)

        @pl.when(index == 5)
        def _():
            last_x(1, (py + 3) % 4)

        @pl.when(index == 6)
        def _():
            last_x(2, (py + 1) % 4)
            last_x(3, (py + 2) % 4)
            shared(3, (px + 2) % 4)

        row_attend(n, sp, xo, bias, ro, qd, kk, vt, gt, mask, mid, mix)

        @pl.when(n == 1)
        def _():
            rows = mix[pl.ds(pl.multiple_of(sp * 512, 512), 512), :].astype(BF16)
            sendbuf[pl.ds(sp * 32, 32)] = rows.reshape(32, 16, 128)

            def scatter(i, carry):
                other = sp * 32 + (here + i) % 32

                @pl.when(other != here)
                def _():
                    remote(sendbuf.at[other], cells.at[here], csend, crecv, (other // RES, other % RES)).start()

                return carry

            lax.fori_loop(0, 32, scatter, 0)

        return carry

    lax.fori_loop(0, 8, attend, 0)
    cells[here] = sendbuf[here]
    for copy in first_z + first_y + second_y:
        copy.wait_send()
    most = bias.at[:, :, :, :, 0]
    remote(most, most, ssend, srecv.at[0], sibling).wait_send()
    most = bias.at[:, pl.ds(0, 3), :, :, 0]
    remote(most, most, hsend, srecv.at[0], sibling).wait_send()
    for name in ("co", "ti", "to", "oi"):
        need(name)
    most = cells.at[pl.ds(0, 127)]
    remote(most, most, csend, crecv, sibling).wait()

    mix[...] = cells[...].reshape(2048, 128).astype(F32)
    wf = oi[...]
    column = 2 * s + r // 8
    is_own = column == r
    chip = r // 2

    def onward_left(a):
        most = lo.at[pl.ds(0, 7), core, a]
        remote(most, most, lsend, lrecv.at[a], sibling).wait_recv()
        line = lo.at[:, core, a]
        remote(line, line, fsend, frecv, sibling).start()

    def residue(a, carry):
        factor = column_step(a, mix, wt.at[1], cw[:, C : 2 * C], co, ti, to, wf, ot)
        fl[a] = factor[:D]
        fr[a] = factor[D:]
        lo[chip, core, a] = factor[:D]

        @pl.when(is_own)
        def _():
            ri[r % 8, a] = factor[D:]

        def send_left(k, carry):
            remote(fl.at[a], lo.at[chip, core, a], lsend, lrecv.at[a], (s, ((chip + k) % 8) * 2 + core)).start()
            return carry

        def send_right(k, carry):
            @pl.when(jnp.logical_not(jnp.logical_and(is_own, k == 0)))
            def _():
                remote(fr.at[a], ri.at[r % 8, a], rsend, rrecv, ((s + k) % 8, column)).start()

            return carry

        lax.fori_loop(1, 8, send_left, 0)
        lax.fori_loop(0, 8, send_right, 0)

        @pl.when(a > 0)
        def _():
            onward_left(a - 1)

        return carry

    lax.fori_loop(0, 4, residue, 0)
    ao[...] = mix[...].astype(BF16)
    save = pltpu.make_async_copy(ao, ao_hbm, lsem.at[0])
    save.start()
    onward_left(3)
    most = lo.at[pl.ds(0, 7), core]
    remote(most, most, lsend, frecv, sibling).wait_send()
    half = lo.at[:, 1 - core]
    remote(half, half, fsend, frecv, sibling).wait()

    @pl.when(is_own)
    def _():
        part = ri.at[pl.ds(0, 7)]
        remote(part, part, rsend, rrecv, sibling).wait()

    @pl.when(jnp.logical_not(is_own))
    def _():
        remote(ri, ri, rsend, rrecv, sibling).wait()

    outer_part(lo, ri, pu, left, wide, block, pairs)
    last = pltpu.make_async_copy(pu, pu_hbm, lsem.at[1])
    last.start()
    last.wait()
    save.wait()


def body(
    alignment,
    pair_state,
    bias_weight,
    row_weight,
    row_output_weight,
    column_weight,
    column_output_weight,
    transition_in,
    transition_out,
    outer_in,
    outer_out,
):
    dma = pltpu.SemaphoreType.DMA
    new, update = pl.pallas_call(
        whole_kernel,
        out_shape=(jax.ShapeDtypeStruct((2048, 128), BF16), jax.ShapeDtypeStruct((2048, 128), BF16)),
        in_specs=[ANY] * 11,
        out_specs=(ANY, ANY),
        scratch_shapes=[
            pltpu.VMEM((64, 32, 128), BF16),
            pltpu.VMEM((8, 128), BF16),
            pltpu.VMEM((C, 4 * C), BF16),
            pltpu.VMEM((C, C), BF16),
            pltpu.VMEM((C, 4 * C), BF16),
            pltpu.VMEM((C, C), BF16),
            pltpu.VMEM((C, 4 * C), BF16),
            pltpu.VMEM((4 * C, C), BF16),
            pltpu.VMEM((64, C), BF16),
            pltpu.VMEM((1024, 128), BF16),
            pltpu.VMEM((4, 32, 128), BF16),
            pltpu.VMEM((16, 2, 32, C), BF16),
            pltpu.VMEM((4, 4, 4, 4, 2, 32, 128), BF16),
            pltpu.VMEM((2, 8, C, 128), BF16),
            pltpu.VMEM((2, 512, C), BF16),
            pltpu.VMEM((2, C, 512), BF16),
            pltpu.VMEM((2, 4, C, 128), BF16),
            pltpu.VMEM((C, 512), BF16),
            pltpu.VMEM((2, 128, 128), F32),
            pltpu.VMEM((2048, 128), F32),
            pltpu.VMEM((2, 3 * C, C), BF16),
            pltpu.VMEM((128, 16, 128), BF16),
            pltpu.VMEM((128, 16, 128), BF16),
            pltpu.VMEM((C, 256), F32),
            pltpu.VMEM((4, D, 256), BF16),
            pltpu.VMEM((4, D, 256), BF16),
            pltpu.VMEM((8, 2, 4, D, 256), BF16),
            pltpu.VMEM((8, 4, D, 256), BF16),
            pltpu.VMEM((2, 2048, 128), F32),
            pltpu.VMEM((512, 4096), BF16),
            pltpu.VMEM((4096, 512), BF16),
            pltpu.VMEM((2048, 128), F32),
            pltpu.VMEM((2048, 128), BF16),
            pltpu.VMEM((2048, 128), BF16),
            dma((3,)),
            dma((3,)),
            dma((4,)),
            dma((4,)),
            dma((4, 4)),
            dma((4,)),
            dma((4,)),
            dma((11,)),
        ]
        + [dma] * 11,
        compiler_params=pltpu.CompilerParams(collective_id=0, has_side_effects=True, vmem_limit_bytes=56 << 20),
        name="evoformer",
    )(
        alignment.reshape(16, 2, 32, C),
        pair_state,
        bias_weight.T,
        row_weight,
        row_output_weight,
        column_weight,
        column_output_weight,
        transition_in,
        transition_out,
        outer_in.T,
        outer_out,
    )
    pair_update = update.reshape(64, 32, 128)
    alignment_out = new.reshape(128, 2, 2, 4, 128).transpose(0, 1, 3, 2, 4).reshape(256, 4, C)
    return (alignment_out, pair_update)


def solution(mesh):
    in_specs = (P("seq", "res", None), P("seq", "res", None)) + (P(),) * 9
    out_specs = (P(None, ("seq", "res"), None), P("seq", "res", None))
    return jax.shard_map(body, mesh=mesh, in_specs=in_specs, out_specs=out_specs, check_vma=False)
```

```python
import functools

import jax
import jax.numpy as jnp
from jax import lax
from jax.experimental import pallas as pl
from jax.experimental.pallas import tpu as pltpu
from jax.sharding import PartitionSpec as P

H = 8
D = 32
C = 256
SEQ = 8
RES = 16
EPS = 1e-05
MESH = pl.DeviceIdType.MESH
F32 = jnp.float32
BF16 = jnp.bfloat16
ANY = pl.BlockSpec(memory_space=pl.ANY)
VMEM = pl.BlockSpec(memory_space=pltpu.VMEM)
NT = (((1,), (1,)), ((), ()))
TN = (((0,), (0,)), ((), ()))


def layer_norm(values):
    center = values - jnp.mean(values, axis=-1, keepdims=True)
    spread = jnp.mean(center * center, axis=-1, keepdims=True)
    return center * lax.rsqrt(spread + EPS)


def dot(a, b):
    return jnp.dot(a, b, preferred_element_type=F32)


def dot_nt(a, b):
    return lax.dot_general(a, b, NT, preferred_element_type=F32)


def dot_tn(a, b):
    return lax.dot_general(a, b, TN, preferred_element_type=F32)


def project(x, wt, wk):
    proj = dot_nt(wt, x)
    q = (proj[:C] * D ** (-0.5)).astype(BF16)
    v = proj[C : 2 * C].astype(BF16)
    g = jax.nn.sigmoid(proj[2 * C :]).astype(BF16)
    k = dot(x, wk).astype(BF16)
    return q, k, v, g


def device(x, y, z, core):
    return (x * 2 + y // 2, (y % 2) * 8 + z * 2 + core)


def remote(src, dst, send, recv, target):
    return pltpu.make_async_remote_copy(
        src_ref=src, dst_ref=dst, send_sem=send, recv_sem=recv, device_id=target, device_id_type=MESH
    )


def pair_bias(pair_ref, weight_ref, out_ref):
    lane = lax.broadcasted_iota(jnp.int32, (32, 512), 1) % 64
    narrow = weight_ref[...].astype(F32)
    weight = jnp.concatenate([jnp.broadcast_to(narrow[h : h + 1], (64, 128)) for h in range(8)], axis=0).astype(BF16)

    def step(k, total):
        rows = pair_ref[pl.ds(k * 8, 8)].reshape(256, 128).astype(F32)
        spread = dot_nt(layer_norm(rows).astype(BF16), weight)
        for one in range(8):
            total = jnp.where(lane == k * 8 + one, spread[one * 32 : one * 32 + 32], total)
        return total

    total = lax.fori_loop(0, 8, step, jnp.zeros((32, 512), F32)).astype(BF16)
    for t in range(4):
        out_ref[t] = total[:, t * 128 : t * 128 + 128]


def row_project(n, x_ref, wt, wk, qd, kk, vt, gt):
    low = lax.broadcasted_iota(jnp.int32, (C, 128), 1) < 64
    x = x_ref[:, n].reshape(512, C).astype(F32)
    q, k, v, g = project(layer_norm(x).astype(BF16), wt[...], wk)
    kk[n] = k
    vt[n] = v
    for t in range(4):
        gt[n, t] = g[:, t * 128 : t * 128 + 128]
        tile = q[:, t * 128 : t * 128 + 128].astype(F32)
        other = pltpu.roll(tile, 64, axis=1)
        qd[n, 2 * t] = jnp.where(low, tile, other).astype(BF16)
        qd[n, 2 * t + 1] = jnp.where(low, other, tile).astype(BF16)


def row_attend(sp, dx, x_ref, bias_ref, wo, qd, kk, vt, gt, mask, mid, mix):
    low = lax.broadcasted_iota(jnp.int32, (D, 128), 1) < 64
    bias = jnp.concatenate(
        [bias_ref[t, dx, 2 * e : 2 * e + 2].reshape(512, 128) for e in range(2) for t in range(4)], axis=1
    ).astype(F32)
    for n in range(2):
        wide = jnp.concatenate([jnp.concatenate([qd[n, sp * 2 + e]] * 4, axis=1) * mask[...] for e in range(2)], axis=1)
        score = dot(kk[n], wide) + bias
        peak = jnp.max(score, axis=0, keepdims=True)
        terms = jnp.exp(score - peak)
        scale = 1.0 / jnp.sum(terms, axis=0, keepdims=True)
        terms = terms.astype(BF16)
        halves = []
        for e in range(2):
            parts = []
            for half in range(2):
                at = e * 512 + half * 256
                o = dot(vt[n, half * 128 : half * 128 + 128, :], terms[:, at : at + 256]) * scale[:, at : at + 256]
                for h in range(4):
                    part = o[h * D : h * D + D, (h // 2) * 128 : (h // 2) * 128 + 128]
                    if h % 2 != e:
                        part = pltpu.roll(part, 64, axis=1)
                    parts.append(part)
            halves.append(parts)
        ot = jnp.concatenate([jnp.where(low, a, b) for a, b in zip(*halves)], axis=0)
        gated = (gt[n, sp].astype(F32) * ot).astype(BF16)
        x = x_ref[pl.ds(sp * 4, 4), n].reshape(128, C).astype(F32)
        new = x + dot_tn(gated, wo[...])
        for ch in range(2):
            mid[n, ch] = new[:, ch * 128 : ch * 128 + 128]
        for ch in range(2):
            for a in range(4):
                mix[pl.ds(sp * 512 + n * 8 + ch * 4 + a, 32, stride=16), :] = mid[n, ch, pl.ds(a, 32, stride=4), :]


def column_step(a, mix, wt, wk, wo, win, wout, wf):
    head = lax.broadcasted_iota(jnp.int32, (C, C), 0) // D
    cells = jnp.concatenate(
        [
            jnp.concatenate([mix[pl.ds(n * 8 + ch * 4 + a, 128, stride=16), :] for ch in range(2)], axis=1)
            for n in range(2)
        ],
        axis=0,
    )
    q, k, v, g = project(layer_norm(cells).astype(BF16), wt[...], wk)
    wide = jnp.concatenate([jnp.where(head == h, q, jnp.zeros_like(q)) for h in range(H)], axis=1)
    score = dot(k, wide)
    peak = jnp.max(score, axis=0, keepdims=True)
    terms = jnp.exp(score - peak)
    scale = 1.0 / jnp.sum(terms, axis=0, keepdims=True)
    terms = terms.astype(BF16)
    ot = jnp.concatenate(
        [dot(v[h * D : h * D + D], terms[:, h * C : h * C + C]) * scale[:, h * C : h * C + C] for h in range(H)], axis=0
    )
    gated = (g.astype(F32) * ot).astype(BF16)
    stream = cells + dot_tn(gated, wo[...])
    normed = layer_norm(stream).astype(BF16)
    hidden = jnp.maximum(dot(normed, win[...]), 0.0).astype(BF16)
    new = (stream + dot(hidden, wout[...])).astype(BF16).astype(F32)
    for n in range(2):
        for ch in range(2):
            mix[pl.ds(n * 8 + ch * 4 + a, 128, stride=16), :] = new[
                n * 128 : n * 128 + 128, ch * 128 : ch * 128 + 128
            ]
    return dot_nt(wf, layer_norm(new).astype(BF16)).astype(BF16)


def outer_weight(w_ref, block):
    block[...] = jnp.zeros_like(block)
    for c in range(32):
        one = w_ref[c * 32 : c * 32 + 32, :]
        for j in range(4):
            block[c * 128 + j * 32 : c * 128 + j * 32 + 32, j * 128 : j * 128 + 128] = one


def outer_part(left_ref, right_ref, out_ref, left, wide, block, pairs):
    for n in range(2):
        left[n] = left_ref[:, :, :, :, n * 128 : n * 128 + 128].reshape(2048, 128).astype(F32)
    right = right_ref[...].reshape(1024, 256)
    for c in range(0, 32, 2):
        rows = jnp.concatenate(
            [
                jnp.concatenate([left[n, pl.ds(c + k, 64, stride=32), :] for n in range(2)], axis=1)
                for k in range(2)
            ],
            axis=0,
        )
        product = (dot_nt(rows.astype(BF16), right) * (1.0 / 256)).astype(BF16)
        for k in range(2):
            for g in range(8):
                wide[g * 64 : g * 64 + 64, (c + k) * 128 : (c + k) * 128 + 128] = product[
                    k * 64 : k * 64 + 64, g * 128 : g * 128 + 128
                ]
    update = dot(wide[...], block[...])
    for g in range(8):
        for j in range(4):
            pairs[pl.ds(g * 4 + j, 64, stride=32), :] = update[g * 64 : g * 64 + 64, j * 128 : j * 128 + 128]
    out_ref[...] = pairs[...].astype(BF16)


def whole_kernel(
    x_hbm, pair_hbm, bw_hbm, rw_hbm, ro_hbm, cw_hbm, co_hbm, ti_hbm, to_hbm, oi_hbm, oo_hbm,
    ao_hbm, pu_hbm,
    pair, bw, rw, ro, cw, co, ti, to, oi, oo,
    own, xo, bias, qd, kk, vt, gt, mask, mid, mix, wt, sendbuf, cells, fl, fr, lo, ri, left, wide, block, pairs,
    ao, pu,
    zsend, zrecv, ysend, yrecv, tsend, trecv, hrecv, srecv, lrecv, lsem,
    hsend, ssend, xsend, xrecv, csend, crecv, lsend, fsend, frecv, rsend, rrecv,
):
    s, r = lax.axis_index("seq"), lax.axis_index("res")
    here = s * RES + r
    pos = {"x": s // 2, "y": (s % 2) * 2 + r // 8, "z": (r % 8) // 2}
    core = r % 2
    sibling = (s, r + 1 - 2 * core)

    def near(dim, by):
        at = dict(pos)
        at[dim] = (pos[dim] + by) % 4
        return device(at["x"], at["y"], at["z"], core)

    loads = {}
    for k, (name, src, dst) in enumerate(
        (
            ("pair", pair_hbm, pair), ("bw", bw_hbm, bw), ("rw", rw_hbm, rw), ("ro", ro_hbm, ro), ("cw", cw_hbm, cw),
            ("co", co_hbm, co), ("ti", ti_hbm, ti), ("to", to_hbm, to), ("oi", oi_hbm, oi), ("oo", oo_hbm, oo),
            ("keep", x_hbm.at[r], xo.at[r]),
        )
    ):
        loads[name] = pltpu.make_async_copy(src, dst, lsem.at[k])
        loads[name].start()

    def need(name):
        loads.pop(name).wait()

    barrier = pltpu.get_barrier_semaphore()

    def greet(k, carry):
        pl.semaphore_signal(barrier, inc=1, device_id=(s, (r + k) % 16), device_id_type=MESH)
        return carry

    lax.fori_loop(1, 16, greet, 0)
    for dim in "xy":
        for by in (1, 2, 3):
            pl.semaphore_signal(barrier, inc=1, device_id=near(dim, by), device_id_type=MESH)

    need("pair")
    need("bw")
    pair_bias(pair, bw, own)
    mine_at = bias.at[:, 0, pos["y"], pos["z"], core]
    place = pltpu.make_async_copy(own, mine_at, lsem.at[0])
    place.start()
    pl.semaphore_wait(barrier, 21)

    def scatter_x(y_lo, first):
        def one(k, carry):
            other = y_lo * 8 + (r + k) % 8
            remote(x_hbm.at[other], xo.at[r], xsend, xrecv, (s, other)).start()
            return carry

        lax.fori_loop(first, 8, one, 0)

    px, py, pz = pos["x"], pos["y"], pos["z"]
    ALL, MOST = pl.ds(0, 4), pl.ds(0, 3)
    REST = pl.ds(1, 3)
    HALVES = (pl.ds(0, 2), pl.ds(2, 2))

    def line(dx, y, ts=MOST, zs=ALL):
        return bias.at[ts, dx, y, zs, core]

    def share(group, what):
        remote(what, what, ssend, srecv.at[group], sibling).start()

    def along_x(k, y):
        for way, by in enumerate((1, 3)):
            remote(line(0, y), line(4 - by, y), hsend, hrecv.at[k, way], near("x", by)).start()

    def onward_x(k, y):
        for way, by in enumerate((1, 3)):
            got = line(4 - by, y)
            remote(got, got, hsend, hrecv.at[k, way], near("x", by)).wait_recv()
            remote(
                line(4 - by, y, zs=HALVES[way]), line(2, y, zs=HALVES[way]), hsend, hrecv.at[k, 2 + way], near("x", by)
            ).start()
            share(4 - by, got)

    def last_x(k, y):
        for way, by in enumerate((1, 3)):
            part = line(2, y, zs=HALVES[way])
            remote(part, part, hsend, hrecv.at[k, 2 + way], near("x", by)).wait_recv()
        share(2, line(2, y))

    def shared(group):
        half = bias.at[ALL, 0, :, :, 1 - core] if group == 0 else bias.at[MOST, group, :, :, 1 - core]
        if group == 4:
            half = bias.at[3, REST, :, :, 1 - core]
        remote(half, half, hsend, srecv.at[group], sibling).wait_recv()

    def start(copies):
        for copy in copies:
            copy.start()
        return copies

    def arrived(copies):
        for copy in copies:
            copy.wait_recv()

    BY = (1, 3, 2)
    first_z = start(
        [remote(own, bias.at[:, 0, py, pz, core], zsend.at[k], zrecv.at[k], near("z", by)) for k, by in enumerate(BY)]
    )
    t_x = start(
        [
            remote(own.at[3], bias.at[3, 4 - by, py, pz, core], tsend.at[k], trecv.at[k], near("x", by))
            for k, by in enumerate(BY)
        ]
    )
    y_lo = r // 8
    scatter_x(y_lo, 1)

    row = lax.broadcasted_iota(jnp.int32, (C, 512), 0) // D
    lane = lax.broadcasted_iota(jnp.int32, (C, 512), 1) // 64
    mask[...] = jnp.where(row == lane, 1.0, 0.0).astype(BF16)
    need("rw")
    for i, at in enumerate((0, 2, 3)):
        wt[0, i * C : i * C + C, :] = rw[:, at * C : at * C + C].T

    place.wait()
    arrived(first_z)
    whole = line(0, py, ALL)
    first_y = start([remote(whole, whole, ysend.at[k], yrecv.at[k], near("y", by)) for k, by in enumerate((1, 3))])
    along_x(0, py)
    share(0, whole)
    scatter_x(1 - y_lo, 0)
    arrived(t_x)
    spot = bias.at[3, REST, py, pz, core]
    t_y = start([remote(spot, spot, tsend.at[3 + k], trecv.at[3 + k], near("y", by)) for k, by in enumerate(BY)])
    need("cw")
    for i, at in enumerate((0, 2, 3)):
        wt[1, i * C : i * C + C, :] = cw[:, at * C : at * C + C].T
    second_y = []
    for k, by in enumerate((1, 3)):
        first_y[k].wait_recv()
        y = (py + 4 - by) % 4
        part = line(0, y, HALVES[k])
        second_y += start([remote(part, part, ysend.at[2 + k], yrecv.at[2 + k], near("y", by))])
        along_x(1 + k, y)
        share(0, line(0, y, ALL))
    need("oo")
    outer_weight(oo, block)
    arrived(t_y)

    def wall(z, ys=ALL):
        return bias.at[3, REST, ys, z, core]

    t_z = start(
        [remote(wall(pz), wall(pz), tsend.at[6 + k], trecv.at[6 + k], near("z", by)) for k, by in enumerate((1, 3))]
    )
    share(4, wall(pz))
    onward_x(0, py)
    arrived(second_y)
    along_x(3, (py + 2) % 4)
    share(0, line(0, (py + 2) % 4, ALL))
    need("keep")
    most = xo.at[pl.ds(0, 15)]
    remote(most, most, xsend, xrecv, sibling).wait()
    row_project(0, xo, wt.at[0], rw[:, C : 2 * C], qd, kk, vt, gt)
    onward_x(1, (py + 3) % 4)
    onward_x(2, (py + 1) % 4)
    for k, by in enumerate((1, 3)):
        t_z[k].wait_recv()
        z = (pz + 4 - by) % 4
        part = wall(z, HALVES[k])
        t_z += start([remote(part, part, tsend.at[8 + k], trecv.at[8 + k], near("z", by))])
        share(4, wall(z))
    row_project(1, xo, wt.at[0], rw[:, C : 2 * C], qd, kk, vt, gt)
    arrived(t_z[2:])
    share(4, wall((pz + 2) % 4))
    need("ro")

    def attend(q, carry):
        dx = q - q // 2 + 2 * (q % 2) * (1 - q // 2)
        sp = (px + dx) % 4

        @pl.when(q == 0)
        def _():
            shared(0)

        @pl.when(q == 1)
        def _():
            onward_x(3, (py + 2) % 4)
            shared(4)
            shared(3)

        @pl.when(q == 2)
        def _():
            last_x(0, py)
            last_x(1, (py + 3) % 4)
            shared(1)

        @pl.when(q == 3)
        def _():
            last_x(2, (py + 1) % 4)
            last_x(3, (py + 2) % 4)
            shared(2)

        row_attend(sp, dx, xo, bias, ro, qd, kk, vt, gt, mask, mid, mix)
        rows = mix[pl.ds(pl.multiple_of(sp * 512, 512), 512), :].astype(BF16)
        sendbuf[pl.ds(sp * 32, 32)] = rows.reshape(32, 16, 128)

        def scatter(i, carry):
            other = sp * 32 + (here + i) % 32

            @pl.when(other != here)
            def _():
                remote(sendbuf.at[other], cells.at[here], csend, crecv, (other // RES, other % RES)).start()

            return carry

        lax.fori_loop(0, 32, scatter, 0)
        return carry

    lax.fori_loop(0, 4, attend, 0)
    cells[here] = sendbuf[here]
    for copy in first_z + first_y + second_y + t_x + t_y + t_z:
        copy.wait_send()
    most = bias.at[:, :, :, :, 0]
    remote(most, most, ssend, srecv.at[0], sibling).wait_send()
    most = bias.at[MOST, MOST, :, :, 0]
    remote(most, most, hsend, srecv.at[0], sibling).wait_send()
    for name in ("co", "ti", "to", "oi"):
        need(name)
    most = cells.at[pl.ds(0, 127)]
    remote(most, most, csend, crecv, sibling).wait()

    mix[...] = cells[...].reshape(2048, 128).astype(F32)
    wf = oi[...]
    column = 2 * s + r // 8
    is_own = column == r
    chip = r // 2

    def onward_left(a):
        most = lo.at[pl.ds(0, 7), core, a]
        remote(most, most, lsend, lrecv.at[a], sibling).wait_recv()
        line = lo.at[:, core, a]
        remote(line, line, fsend, frecv, sibling).start()

    def residue(a, carry):
        factor = column_step(a, mix, wt.at[1], cw[:, C : 2 * C], co, ti, to, wf)
        fl[a] = factor[:D]
        fr[a] = factor[D:]
        lo[chip, core, a] = factor[:D]

        @pl.when(is_own)
        def _():
            ri[r % 8, a] = factor[D:]

        def send_left(k, carry):
            remote(fl.at[a], lo.at[chip, core, a], lsend, lrecv.at[a], (s, ((chip + k) % 8) * 2 + core)).start()
            return carry

        def send_right(k, carry):
            @pl.when(jnp.logical_not(jnp.logical_and(is_own, k == 0)))
            def _():
                remote(fr.at[a], ri.at[r % 8, a], rsend, rrecv, ((s + k) % 8, column)).start()

            return carry

        lax.fori_loop(1, 8, send_left, 0)
        lax.fori_loop(0, 8, send_right, 0)

        @pl.when(a > 0)
        def _():
            onward_left(a - 1)

        return carry

    lax.fori_loop(0, 4, residue, 0)
    new = mix[...].astype(BF16).reshape(256, 8, 128)
    for ch in range(2):
        ao[:, :, ch * 128 : ch * 128 + 128] = new[:, ch * 4 : ch * 4 + 4, :]
    save = pltpu.make_async_copy(ao, ao_hbm, lsem.at[0])
    save.start()
    onward_left(3)
    most = lo.at[pl.ds(0, 7), core]
    remote(most, most, lsend, frecv, sibling).wait_send()
    half = lo.at[:, 1 - core]
    remote(half, half, fsend, frecv, sibling).wait()

    @pl.when(is_own)
    def _():
        part = ri.at[pl.ds(0, 7)]
        remote(part, part, rsend, rrecv, sibling).wait()

    @pl.when(jnp.logical_not(is_own))
    def _():
        remote(ri, ri, rsend, rrecv, sibling).wait()

    outer_part(lo, ri, pu, left, wide, block, pairs)
    last = pltpu.make_async_copy(pu, pu_hbm, lsem.at[1])
    last.start()
    last.wait()
    save.wait()


def body(
    alignment,
    pair_state,
    bias_weight,
    row_weight,
    row_output_weight,
    column_weight,
    column_output_weight,
    transition_in,
    transition_out,
    outer_in,
    outer_out,
):
    dma = pltpu.SemaphoreType.DMA
    new, update = pl.pallas_call(
        whole_kernel,
        out_shape=(jax.ShapeDtypeStruct((256, 4, C), BF16), jax.ShapeDtypeStruct((2048, 128), BF16)),
        in_specs=[ANY] * 11,
        out_specs=(ANY, ANY),
        scratch_shapes=[
            pltpu.VMEM((64, 32, 128), BF16),
            pltpu.VMEM((8, 128), BF16),
            pltpu.VMEM((C, 4 * C), BF16),
            pltpu.VMEM((C, C), BF16),
            pltpu.VMEM((C, 4 * C), BF16),
            pltpu.VMEM((C, C), BF16),
            pltpu.VMEM((C, 4 * C), BF16),
            pltpu.VMEM((4 * C, C), BF16),
            pltpu.VMEM((64, C), BF16),
            pltpu.VMEM((1024, 128), BF16),
            pltpu.VMEM((4, 32, 128), BF16),
            pltpu.VMEM((16, 2, 32, C), BF16),
            pltpu.VMEM((4, 4, 4, 4, 2, 32, 128), BF16),
            pltpu.VMEM((2, 8, C, 128), BF16),
            pltpu.VMEM((2, 512, C), BF16),
            pltpu.VMEM((2, C, 512), BF16),
            pltpu.VMEM((2, 4, C, 128), BF16),
            pltpu.VMEM((C, 512), BF16),
            pltpu.VMEM((2, 2, 128, 128), F32),
            pltpu.VMEM((2048, 128), F32),
            pltpu.VMEM((2, 3 * C, C), BF16),
            pltpu.VMEM((128, 16, 128), BF16),
            pltpu.VMEM((128, 16, 128), BF16),
            pltpu.VMEM((4, D, 256), BF16),
            pltpu.VMEM((4, D, 256), BF16),
            pltpu.VMEM((8, 2, 4, D, 256), BF16),
            pltpu.VMEM((8, 4, D, 256), BF16),
            pltpu.VMEM((2, 2048, 128), F32),
            pltpu.VMEM((512, 4096), BF16),
            pltpu.VMEM((4096, 512), BF16),
            pltpu.VMEM((2048, 128), F32),
            pltpu.VMEM((256, 4, C), BF16),
            pltpu.VMEM((2048, 128), BF16),
            dma((3,)),
            dma((3,)),
            dma((4,)),
            dma((4,)),
            dma((10,)),
            dma((10,)),
            dma((4, 4)),
            dma((5,)),
            dma((4,)),
            dma((11,)),
        ]
        + [dma] * 11,
        compiler_params=pltpu.CompilerParams(collective_id=0, has_side_effects=True, vmem_limit_bytes=56 << 20),
        name="evoformer",
    )(
        alignment.reshape(16, 2, 32, C),
        pair_state,
        bias_weight.T,
        row_weight,
        row_output_weight,
        column_weight,
        column_output_weight,
        transition_in,
        transition_out,
        outer_in.T,
        outer_out,
    )
    pair_update = update.reshape(64, 32, 128)
    return (new, pair_update)


def solution(mesh):
    in_specs = (P("seq", "res", None), P("seq", "res", None)) + (P(),) * 9
    out_specs = (P(None, ("seq", "res"), None), P("seq", "res", None))
    return jax.shard_map(body, mesh=mesh, in_specs=in_specs, out_specs=out_specs, check_vma=False)
```

```python
import functools

import jax
import jax.numpy as jnp
from jax import lax
from jax.experimental import pallas as pl
from jax.experimental.pallas import tpu as pltpu
from jax.sharding import PartitionSpec as P

H = 8
D = 32
C = 256
SEQ = 8
RES = 16
EPS = 1e-05
MESH = pl.DeviceIdType.MESH
F32 = jnp.float32
BF16 = jnp.bfloat16
ANY = pl.BlockSpec(memory_space=pl.ANY)
VMEM = pl.BlockSpec(memory_space=pltpu.VMEM)
NT = (((1,), (1,)), ((), ()))
TN = (((0,), (0,)), ((), ()))


def layer_norm(values):
    center = values - jnp.mean(values, axis=-1, keepdims=True)
    spread = jnp.mean(center * center, axis=-1, keepdims=True)
    return center * lax.rsqrt(spread + EPS)


def dot(a, b):
    return jnp.dot(a, b, preferred_element_type=F32)


def dot_nt(a, b):
    return lax.dot_general(a, b, NT, preferred_element_type=F32)


def dot_tn(a, b):
    return lax.dot_general(a, b, TN, preferred_element_type=F32)


def project(x, wt, wk):
    proj = dot_nt(wt, x)
    q = (proj[:C] * D ** (-0.5)).astype(BF16)
    v = proj[C : 2 * C].astype(BF16)
    g = jax.nn.sigmoid(proj[2 * C :]).astype(BF16)
    k = dot(x, wk).astype(BF16)
    return q, k, v, g


def device(x, y, z, core):
    return (x * 2 + y // 2, (y % 2) * 8 + z * 2 + core)


def remote(src, dst, send, recv, target):
    return pltpu.make_async_remote_copy(
        src_ref=src, dst_ref=dst, send_sem=send, recv_sem=recv, device_id=target, device_id_type=MESH
    )


def pair_bias(pair_ref, weight_ref, out_ref):
    lane = lax.broadcasted_iota(jnp.int32, (32, 512), 1) % 64
    narrow = weight_ref[...].astype(F32)
    weight = jnp.concatenate([jnp.broadcast_to(narrow[h : h + 1], (64, 128)) for h in range(8)], axis=0).astype(BF16)

    def step(k, total):
        rows = pair_ref[pl.ds(k * 8, 8)].reshape(256, 128).astype(F32)
        spread = dot_nt(layer_norm(rows).astype(BF16), weight)
        for one in range(8):
            total = jnp.where(lane == k * 8 + one, spread[one * 32 : one * 32 + 32], total)
        return total

    total = lax.fori_loop(0, 8, step, jnp.zeros((32, 512), F32)).astype(BF16)
    for t in range(4):
        out_ref[t] = total[:, t * 128 : t * 128 + 128]


def row_project(n, x_ref, wt, wk, qd, kk, vt, gt):
    low = lax.broadcasted_iota(jnp.int32, (C, 128), 1) < 64
    x = x_ref[:, n].reshape(512, C).astype(F32)
    q, k, v, g = project(layer_norm(x).astype(BF16), wt[...], wk)
    kk[n] = k
    vt[n] = v
    for t in range(4):
        gt[n, t] = g[:, t * 128 : t * 128 + 128]
        tile = q[:, t * 128 : t * 128 + 128].astype(F32)
        other = pltpu.roll(tile, 64, axis=1)
        qd[n, 2 * t] = jnp.where(low, tile, other).astype(BF16)
        qd[n, 2 * t + 1] = jnp.where(low, other, tile).astype(BF16)


def row_attend(sp, dx, x_ref, bias_ref, wo, qd, kk, vt, gt, mask, mid, mix):
    low = lax.broadcasted_iota(jnp.int32, (D, 128), 1) < 64
    bias = jnp.concatenate(
        [bias_ref[t, dx, 2 * e : 2 * e + 2].reshape(512, 128) for e in range(2) for t in range(4)], axis=1
    ).astype(F32)
    for n in range(2):
        wide = jnp.concatenate([jnp.concatenate([qd[n, sp * 2 + e]] * 4, axis=1) * mask[...] for e in range(2)], axis=1)
        score = dot(kk[n], wide) + bias
        peak = jnp.max(score, axis=0, keepdims=True)
        terms = jnp.exp(score - peak)
        scale = 1.0 / jnp.sum(terms, axis=0, keepdims=True)
        terms = terms.astype(BF16)
        halves = []
        for e in range(2):
            parts = []
            for half in range(2):
                at = e * 512 + half * 256
                o = dot(vt[n, half * 128 : half * 128 + 128, :], terms[:, at : at + 256]) * scale[:, at : at + 256]
                for h in range(4):
                    part = o[h * D : h * D + D, (h // 2) * 128 : (h // 2) * 128 + 128]
                    if h % 2 != e:
                        part = pltpu.roll(part, 64, axis=1)
                    parts.append(part)
            halves.append(parts)
        ot = jnp.concatenate([jnp.where(low, a, b) for a, b in zip(*halves)], axis=0)
        gated = (gt[n, sp].astype(F32) * ot).astype(BF16)
        x = x_ref[pl.ds(sp * 4, 4), n].reshape(128, C).astype(F32)
        new = x + dot_tn(gated, wo[...])
        for ch in range(2):
            mid[n, ch] = new[:, ch * 128 : ch * 128 + 128]
        for ch in range(2):
            for a in range(4):
                mix[pl.ds(sp * 512 + n * 8 + ch * 4 + a, 32, stride=16), :] = mid[n, ch, pl.ds(a, 32, stride=4), :]


def column_step(a, mix, wt, wk, wo, win, wout, wf):
    head = lax.broadcasted_iota(jnp.int32, (C, C), 0) // D
    cells = jnp.concatenate(
        [
            jnp.concatenate([mix[pl.ds(n * 8 + ch * 4 + a, 128, stride=16), :] for ch in range(2)], axis=1)
            for n in range(2)
        ],
        axis=0,
    )
    q, k, v, g = project(layer_norm(cells).astype(BF16), wt[...], wk)
    wide = jnp.concatenate([jnp.where(head == h, q, jnp.zeros_like(q)) for h in range(H)], axis=1)
    score = dot(k, wide)
    peak = jnp.max(score, axis=0, keepdims=True)
    terms = jnp.exp(score - peak)
    scale = 1.0 / jnp.sum(terms, axis=0, keepdims=True)
    terms = terms.astype(BF16)
    ot = jnp.concatenate(
        [dot(v[h * D : h * D + D], terms[:, h * C : h * C + C]) * scale[:, h * C : h * C + C] for h in range(H)], axis=0
    )
    gated = (g.astype(F32) * ot).astype(BF16)
    stream = cells + dot_tn(gated, wo[...])
    normed = layer_norm(stream).astype(BF16)
    hidden = jnp.maximum(dot(normed, win[...]), 0.0).astype(BF16)
    new = (stream + dot(hidden, wout[...])).astype(BF16).astype(F32)
    for n in range(2):
        for ch in range(2):
            mix[pl.ds(n * 8 + ch * 4 + a, 128, stride=16), :] = new[
                n * 128 : n * 128 + 128, ch * 128 : ch * 128 + 128
            ]
    return dot_nt(wf, layer_norm(new).astype(BF16)).astype(BF16)


def outer_weight(w_ref, block):
    block[...] = jnp.zeros_like(block)
    for c in range(32):
        one = w_ref[c * 32 : c * 32 + 32, :]
        for j in range(4):
            block[c * 128 + j * 32 : c * 128 + j * 32 + 32, j * 128 : j * 128 + 128] = one


def outer_part(left_ref, right_ref, out_ref, left, wide, block, pairs):
    for n in range(2):
        left[n] = left_ref[:, :, :, :, n * 128 : n * 128 + 128].reshape(2048, 128).astype(F32)
    right = right_ref[...].reshape(1024, 256)
    for c in range(0, 32, 2):
        rows = jnp.concatenate(
            [
                jnp.concatenate([left[n, pl.ds(c + k, 64, stride=32), :] for n in range(2)], axis=1)
                for k in range(2)
            ],
            axis=0,
        )
        product = (dot_nt(rows.astype(BF16), right) * (1.0 / 256)).astype(BF16)
        for k in range(2):
            for g in range(8):
                wide[g * 64 : g * 64 + 64, (c + k) * 128 : (c + k) * 128 + 128] = product[
                    k * 64 : k * 64 + 64, g * 128 : g * 128 + 128
                ]
    update = dot(wide[...], block[...])
    for g in range(8):
        for j in range(4):
            pairs[pl.ds(g * 4 + j, 64, stride=32), :] = update[g * 64 : g * 64 + 64, j * 128 : j * 128 + 128]
    out_ref[...] = pairs[...].astype(BF16)


def whole_kernel(
    x_hbm, pair_hbm, bw_hbm, rw_hbm, ro_hbm, cw_hbm, co_hbm, ti_hbm, to_hbm, oi_hbm, oo_hbm,
    ao_hbm, pu_hbm,
    pair, bw, rw, ro, cw, co, ti, to, oi, oo,
    own, xo, bias, qd, kk, vt, gt, mask, mid, mix, wt, sendbuf, cells, fl, fr, lo, ri, left, wide, block, pairs,
    ao, pu,
    nsend, nrecv, hrecv, srecv, lrecv, lsem,
    hsend, ssend, xsend, xrecv, csend, crecv, lsend, fsend, frecv, rsend, rrecv,
):
    s, r = lax.axis_index("seq"), lax.axis_index("res")
    here = s * RES + r
    pos = {"x": s // 2, "y": (s % 2) * 2 + r // 8, "z": (r % 8) // 2}
    core = r % 2
    sibling = (s, r + 1 - 2 * core)

    def near(dim, by):
        at = dict(pos)
        at[dim] = (pos[dim] + by) % 4
        return device(at["x"], at["y"], at["z"], core)

    loads = {}
    for k, (name, src, dst) in enumerate(
        (
            ("pair", pair_hbm, pair), ("bw", bw_hbm, bw), ("rw", rw_hbm, rw), ("ro", ro_hbm, ro), ("cw", cw_hbm, cw),
            ("co", co_hbm, co), ("ti", ti_hbm, ti), ("to", to_hbm, to), ("oi", oi_hbm, oi), ("oo", oo_hbm, oo),
            ("keep", x_hbm.at[r], xo.at[r]),
        )
    ):
        loads[name] = pltpu.make_async_copy(src, dst, lsem.at[k])
        loads[name].start()

    def need(name):
        loads.pop(name).wait()

    barrier = pltpu.get_barrier_semaphore()

    def greet(k, carry):
        pl.semaphore_signal(barrier, inc=1, device_id=(s, (r + k) % 16), device_id_type=MESH)
        return carry

    lax.fori_loop(1, 16, greet, 0)
    for dim in "xy":
        for by in (1, 2, 3):
            pl.semaphore_signal(barrier, inc=1, device_id=near(dim, by), device_id_type=MESH)

    need("pair")
    need("bw")
    pair_bias(pair, bw, own)
    mine_at = bias.at[:, 0, pos["y"], pos["z"], core]
    place = pltpu.make_async_copy(own, mine_at, lsem.at[0])
    place.start()
    pl.semaphore_wait(barrier, 21)

    def scatter_x(k, carry):
        other = (r + k) % 16
        remote(x_hbm.at[other], xo.at[r], xsend, xrecv, (s, other)).start()
        return carry

    px, py, pz = pos["x"], pos["y"], pos["z"]
    ALL, MOST, REST = pl.ds(0, 4), pl.ds(0, 3), pl.ds(1, 3)
    LOW, HIGH = pl.ds(0, 2), pl.ds(2, 2)
    HALVES = (LOW, HIGH)
    BY = (1, 3, 2)
    PARTS = [(kind, by) for by in (0, 3, 1, 2) for kind in "yz"]

    def part_of(dx, k, inner=ALL):
        kind, by = PARTS[k]
        if kind == "y":
            return bias.at[LOW, dx, (py + by) % 4, inner, core]
        return bias.at[2, dx, inner, (pz + by) % 4, core]

    def share(group, what):
        remote(what, what, ssend, srecv.at[group], sibling).start()

    def along_x(k):
        for way, by in enumerate((1, 3)):
            remote(part_of(0, k), part_of(4 - by, k), hsend, hrecv.at[k, way], near("x", by)).start()

    def onward_x(*ks):
        for k in ks:
            for way, by in enumerate((1, 3)):
                got = part_of(4 - by, k)
                remote(got, got, hsend, hrecv.at[k, way], near("x", by)).wait_recv()
                remote(
                    part_of(4 - by, k, HALVES[way]), part_of(2, k, HALVES[way]), hsend, hrecv.at[k, 2 + way], near("x", by)
                ).start()
                share(4 - by, got)

    def last_x(*ks):
        for k in ks:
            for way, by in enumerate((1, 3)):
                half = part_of(2, k, HALVES[way])
                remote(half, half, hsend, hrecv.at[k, 2 + way], near("x", by)).wait_recv()
            share(2, part_of(2, k))

    def shared(group):
        half = bias.at[ALL, 0, :, :, 1 - core] if group == 0 else bias.at[MOST, group, :, :, 1 - core]
        if group == 4:
            half = bias.at[3, REST, :, :, 1 - core]
        remote(half, half, hsend, srecv.at[group], sibling).wait_recv()

    copies = []

    def three(dim, src, dst, base):
        made = [remote(src, dst, nsend.at[base + k], nrecv.at[base + k], near(dim, by)) for k, by in enumerate(BY)]
        for copy in made:
            copy.start()
        copies.extend(made)
        return made

    def arrived(made):
        for copy in made:
            copy.wait_recv()

    low_z = three("z", own.at[LOW], bias.at[LOW, 0, py, pz, core], 0)
    high_y = three("y", own.at[HIGH], bias.at[HIGH, 0, py, pz, core], 3)
    t_x = []
    for k, by in enumerate(BY):
        t_x.append(remote(own.at[3], bias.at[3, 4 - by, py, pz, core], nsend.at[6 + k], nrecv.at[6 + k], near("x", by)))
        t_x[k].start()
    copies.extend(t_x)
    lax.fori_loop(1, 16, scatter_x, 0)

    place.wait()
    arrived(low_z)
    mine = bias.at[LOW, 0, py, :, core]
    low_y = three("y", mine, mine, 9)
    along_x(0)
    arrived(high_y)
    mine = bias.at[HIGH, 0, :, pz, core]
    high_z = three("z", mine, mine, 12)
    along_x(1)
    arrived(t_x)
    mine = bias.at[3, REST, py, pz, core]
    t_y = three("y", mine, mine, 15)
    row = lax.broadcasted_iota(jnp.int32, (C, 512), 0) // D
    lane = lax.broadcasted_iota(jnp.int32, (C, 512), 1) // 64
    mask[...] = jnp.where(row == lane, 1.0, 0.0).astype(BF16)
    need("rw")
    for i, at in enumerate((0, 2, 3)):
        wt[0, i * C : i * C + C, :] = rw[:, at * C : at * C + C].T
    for k in range(3):
        low_y[k].wait_recv()
        along_x(2 + 2 * k)
        high_z[k].wait_recv()
        along_x(3 + 2 * k)
        if k == 0:
            onward_x(0, 1)
    share(0, bias.at[:, 0, :, :, core])
    arrived(t_y)
    mine = bias.at[3, REST, :, pz, core]
    t_z = three("z", mine, mine, 18)
    need("keep")
    most = xo.at[pl.ds(0, 15)]
    remote(most, most, xsend, xrecv, sibling).wait()
    row_project(0, xo, wt.at[0], rw[:, C : 2 * C], qd, kk, vt, gt)
    onward_x(2, 3)
    row_project(1, xo, wt.at[0], rw[:, C : 2 * C], qd, kk, vt, gt)
    onward_x(4, 5)
    need("oo")
    outer_weight(oo, block)
    need("cw")
    for i, at in enumerate((0, 2, 3)):
        wt[1, i * C : i * C + C, :] = cw[:, at * C : at * C + C].T
    arrived(t_z)
    share(4, bias.at[3, REST, :, :, core])
    need("ro")

    def attend(q, carry):
        dx = q - q // 2 + 2 * (q % 2) * (1 - q // 2)
        sp = (px + dx) % 4

        @pl.when(q == 0)
        def _():
            shared(0)

        @pl.when(q == 1)
        def _():
            onward_x(6, 7)
            last_x(0, 1)
            shared(4)
            shared(3)

        @pl.when(q == 2)
        def _():
            last_x(2, 3, 4, 5)
            shared(1)

        @pl.when(q == 3)
        def _():
            last_x(6, 7)
            shared(2)

        row_attend(sp, dx, xo, bias, ro, qd, kk, vt, gt, mask, mid, mix)
        rows = mix[pl.ds(pl.multiple_of(sp * 512, 512), 512), :].astype(BF16)
        sendbuf[pl.ds(sp * 32, 32)] = rows.reshape(32, 16, 128)

        for yh in range(2):
            to_s = sp * 2 + yh

            def scatter(i, carry):
                to_r = lax.bitwise_and(r + i, 15)
                other = to_s * 16 + to_r

                @pl.when(other != here)
                def _():
                    remote(sendbuf.at[other], cells.at[here], csend, crecv, (to_s, to_r)).start()

                return carry

            lax.fori_loop(0, 16, scatter, 0, unroll=True)
        return carry

    lax.fori_loop(0, 4, attend, 0)
    cells[here] = sendbuf[here]
    for copy in copies:
        copy.wait_send()
    most = bias.at[:, :, :, :, 0]
    remote(most, most, ssend, srecv.at[0], sibling).wait_send()
    most = bias.at[MOST, MOST, :, :, 0]
    remote(most, most, hsend, srecv.at[0], sibling).wait_send()
    for name in ("co", "ti", "to", "oi"):
        need(name)
    most = cells.at[pl.ds(0, 127)]
    remote(most, most, csend, crecv, sibling).wait()

    mix[...] = cells[...].reshape(2048, 128).astype(F32)
    wf = oi[...]
    column = 2 * s + r // 8
    is_own = column == r
    chip = r // 2

    def onward_left(a):
        most = lo.at[pl.ds(0, 7), core, a]
        remote(most, most, lsend, lrecv.at[a], sibling).wait_recv()
        line = lo.at[:, core, a]
        remote(line, line, fsend, frecv, sibling).start()

    def residue(a, carry):
        factor = column_step(a, mix, wt.at[1], cw[:, C : 2 * C], co, ti, to, wf)
        fl[a] = factor[:D]
        fr[a] = factor[D:]
        lo[chip, core, a] = factor[:D]

        @pl.when(is_own)
        def _():
            ri[r % 8, a] = factor[D:]

        def send_left(k, carry):
            remote(fl.at[a], lo.at[chip, core, a], lsend, lrecv.at[a], (s, lax.bitwise_and(chip + k, 7) * 2 + core)).start()
            return carry

        def send_right(k, carry):
            @pl.when(jnp.logical_not(jnp.logical_and(is_own, k == 0)))
            def _():
                remote(fr.at[a], ri.at[r % 8, a], rsend, rrecv, (lax.bitwise_and(s + k, 7), column)).start()

            return carry

        lax.fori_loop(1, 8, send_left, 0, unroll=True)
        lax.fori_loop(0, 8, send_right, 0, unroll=True)

        @pl.when(a > 0)
        def _():
            onward_left(a - 1)

        return carry

    lax.fori_loop(0, 4, residue, 0)
    new = mix[...].astype(BF16).reshape(256, 8, 128)
    for ch in range(2):
        ao[:, :, ch * 128 : ch * 128 + 128] = new[:, ch * 4 : ch * 4 + 4, :]
    save = pltpu.make_async_copy(ao, ao_hbm, lsem.at[0])
    save.start()
    onward_left(3)
    most = lo.at[pl.ds(0, 7), core]
    remote(most, most, lsend, frecv, sibling).wait_send()
    half = lo.at[:, 1 - core]
    remote(half, half, fsend, frecv, sibling).wait()

    @pl.when(is_own)
    def _():
        part = ri.at[pl.ds(0, 7)]
        remote(part, part, rsend, rrecv, sibling).wait()

    @pl.when(jnp.logical_not(is_own))
    def _():
        remote(ri, ri, rsend, rrecv, sibling).wait()

    outer_part(lo, ri, pu, left, wide, block, pairs)
    last = pltpu.make_async_copy(pu, pu_hbm, lsem.at[1])
    last.start()
    last.wait()
    save.wait()


def body(
    alignment,
    pair_state,
    bias_weight,
    row_weight,
    row_output_weight,
    column_weight,
    column_output_weight,
    transition_in,
    transition_out,
    outer_in,
    outer_out,
):
    dma = pltpu.SemaphoreType.DMA
    new, update = pl.pallas_call(
        whole_kernel,
        out_shape=(jax.ShapeDtypeStruct((256, 4, C), BF16), jax.ShapeDtypeStruct((2048, 128), BF16)),
        in_specs=[ANY] * 11,
        out_specs=(ANY, ANY),
        scratch_shapes=[
            pltpu.VMEM((64, 32, 128), BF16),
            pltpu.VMEM((8, 128), BF16),
            pltpu.VMEM((C, 4 * C), BF16),
            pltpu.VMEM((C, C), BF16),
            pltpu.VMEM((C, 4 * C), BF16),
            pltpu.VMEM((C, C), BF16),
            pltpu.VMEM((C, 4 * C), BF16),
            pltpu.VMEM((4 * C, C), BF16),
            pltpu.VMEM((64, C), BF16),
            pltpu.VMEM((1024, 128), BF16),
            pltpu.VMEM((4, 32, 128), BF16),
            pltpu.VMEM((16, 2, 32, C), BF16),
            pltpu.VMEM((4, 4, 4, 4, 2, 32, 128), BF16),
            pltpu.VMEM((2, 8, C, 128), BF16),
            pltpu.VMEM((2, 512, C), BF16),
            pltpu.VMEM((2, C, 512), BF16),
            pltpu.VMEM((2, 4, C, 128), BF16),
            pltpu.VMEM((C, 512), BF16),
            pltpu.VMEM((2, 2, 128, 128), F32),
            pltpu.VMEM((2048, 128), F32),
            pltpu.VMEM((2, 3 * C, C), BF16),
            pltpu.VMEM((128, 16, 128), BF16),
            pltpu.VMEM((128, 16, 128), BF16),
            pltpu.VMEM((4, D, 256), BF16),
            pltpu.VMEM((4, D, 256), BF16),
            pltpu.VMEM((8, 2, 4, D, 256), BF16),
            pltpu.VMEM((8, 4, D, 256), BF16),
            pltpu.VMEM((2, 2048, 128), F32),
            pltpu.VMEM((512, 4096), BF16),
            pltpu.VMEM((4096, 512), BF16),
            pltpu.VMEM((2048, 128), F32),
            pltpu.VMEM((256, 4, C), BF16),
            pltpu.VMEM((2048, 128), BF16),
            dma((21,)),
            dma((21,)),
            dma((8, 4)),
            dma((5,)),
            dma((4,)),
            dma((11,)),
        ]
        + [dma] * 11,
        compiler_params=pltpu.CompilerParams(collective_id=0, has_side_effects=True, vmem_limit_bytes=56 << 20),
        name="evoformer",
    )(
        alignment.reshape(16, 2, 32, C),
        pair_state,
        bias_weight.T,
        row_weight,
        row_output_weight,
        column_weight,
        column_output_weight,
        transition_in,
        transition_out,
        outer_in.T,
        outer_out,
    )
    pair_update = update.reshape(64, 32, 128)
    return (new, pair_update)


def solution(mesh):
    in_specs = (P("seq", "res", None), P("seq", "res", None)) + (P(),) * 9
    out_specs = (P(None, ("seq", "res"), None), P("seq", "res", None))
    return jax.shard_map(body, mesh=mesh, in_specs=in_specs, out_specs=out_specs, check_vma=False)
```

```python
import functools

import jax
import jax.numpy as jnp
from jax import lax
from jax.experimental import pallas as pl
from jax.experimental.pallas import tpu as pltpu
from jax.sharding import PartitionSpec as P

H = 8
D = 32
C = 256
SEQ = 8
RES = 16
EPS = 1e-05
MESH = pl.DeviceIdType.MESH
F32 = jnp.float32
BF16 = jnp.bfloat16
ANY = pl.BlockSpec(memory_space=pl.ANY)
VMEM = pl.BlockSpec(memory_space=pltpu.VMEM)
NT = (((1,), (1,)), ((), ()))
TN = (((0,), (0,)), ((), ()))


def layer_norm(values):
    center = values - jnp.mean(values, axis=-1, keepdims=True)
    spread = jnp.mean(center * center, axis=-1, keepdims=True)
    return center * lax.rsqrt(spread + EPS)


def dot(a, b):
    return jnp.dot(a, b, preferred_element_type=F32)


def dot_nt(a, b):
    return lax.dot_general(a, b, NT, preferred_element_type=F32)


def dot_tn(a, b):
    return lax.dot_general(a, b, TN, preferred_element_type=F32)


def project(x, wt, wk):
    proj = dot_nt(wt, x)
    q = (proj[:C] * D ** (-0.5)).astype(BF16)
    v = proj[C : 2 * C].astype(BF16)
    g = jax.nn.sigmoid(proj[2 * C :]).astype(BF16)
    k = dot(x, wk).astype(BF16)
    return q, k, v, g


def device(x, y, z, core):
    return (x * 2 + y // 2, (y % 2) * 8 + z * 2 + core)


def remote(src, dst, send, recv, target):
    return pltpu.make_async_remote_copy(
        src_ref=src, dst_ref=dst, send_sem=send, recv_sem=recv, device_id=target, device_id_type=MESH
    )


def pair_bias(pair_ref, weight_ref, out_ref):
    lane = lax.broadcasted_iota(jnp.int32, (32, 512), 1) % 64
    narrow = weight_ref[...].astype(F32)
    weight = jnp.concatenate([jnp.broadcast_to(narrow[h : h + 1], (64, 128)) for h in range(8)], axis=0).astype(BF16)

    def step(k, total):
        rows = pair_ref[pl.ds(k * 8, 8)].reshape(256, 128).astype(F32)
        spread = dot_nt(layer_norm(rows).astype(BF16), weight)
        for one in range(8):
            total = jnp.where(lane == k * 8 + one, spread[one * 32 : one * 32 + 32], total)
        return total

    total = lax.fori_loop(0, 8, step, jnp.zeros((32, 512), F32)).astype(BF16)
    for t in range(4):
        out_ref[t] = total[:, t * 128 : t * 128 + 128]


def row_project(n, x_ref, wt, wk, qd, kk, vt, gt):
    low = lax.broadcasted_iota(jnp.int32, (C, 128), 1) < 64
    x = x_ref[:, n].reshape(512, C).astype(F32)
    q, k, v, g = project(layer_norm(x).astype(BF16), wt[...], wk)
    kk[n] = k
    vt[n] = v
    for t in range(4):
        gt[n, t] = g[:, t * 128 : t * 128 + 128]
        tile = q[:, t * 128 : t * 128 + 128].astype(F32)
        other = pltpu.roll(tile, 64, axis=1)
        qd[n, 2 * t] = jnp.where(low, tile, other).astype(BF16)
        qd[n, 2 * t + 1] = jnp.where(low, other, tile).astype(BF16)


def row_attend(sp, dx, x_ref, bias_ref, wo, qd, kk, vt, gt, mask, mid, mix):
    low = lax.broadcasted_iota(jnp.int32, (D, 128), 1) < 64
    bias = jnp.concatenate(
        [bias_ref[t, dx, 2 * e : 2 * e + 2].reshape(512, 128) for e in range(2) for t in range(4)], axis=1
    ).astype(F32)
    for n in range(2):
        wide = jnp.concatenate([jnp.concatenate([qd[n, sp * 2 + e]] * 4, axis=1) * mask[...] for e in range(2)], axis=1)
        score = dot(kk[n], wide) + bias
        peak = jnp.max(score, axis=0, keepdims=True)
        terms = jnp.exp(score - peak)
        scale = 1.0 / jnp.sum(terms, axis=0, keepdims=True)
        terms = terms.astype(BF16)
        halves = []
        for e in range(2):
            parts = []
            for half in range(2):
                at = e * 512 + half * 256
                o = dot(vt[n, half * 128 : half * 128 + 128, :], terms[:, at : at + 256]) * scale[:, at : at + 256]
                for h in range(4):
                    part = o[h * D : h * D + D, (h // 2) * 128 : (h // 2) * 128 + 128]
                    if h % 2 != e:
                        part = pltpu.roll(part, 64, axis=1)
                    parts.append(part)
            halves.append(parts)
        ot = jnp.concatenate([jnp.where(low, a, b) for a, b in zip(*halves)], axis=0)
        gated = (gt[n, sp].astype(F32) * ot).astype(BF16)
        x = x_ref[pl.ds(sp * 4, 4), n].reshape(128, C).astype(F32)
        new = x + dot_tn(gated, wo[...])
        for ch in range(2):
            mid[n, ch] = new[:, ch * 128 : ch * 128 + 128]
        for ch in range(2):
            for a in range(4):
                mix[pl.ds(sp * 512 + n * 8 + ch * 4 + a, 32, stride=16), :] = mid[n, ch, pl.ds(a, 32, stride=4), :]


def column_step(a, mix, wt, wk, wo, win, wout, wf):
    head = lax.broadcasted_iota(jnp.int32, (C, C), 0) // D
    cells = jnp.concatenate(
        [
            jnp.concatenate([mix[pl.ds(n * 8 + ch * 4 + a, 128, stride=16), :] for ch in range(2)], axis=1)
            for n in range(2)
        ],
        axis=0,
    )
    q, k, v, g = project(layer_norm(cells).astype(BF16), wt[...], wk)
    wide = jnp.concatenate([jnp.where(head == h, q, jnp.zeros_like(q)) for h in range(H)], axis=1)
    score = dot(k, wide)
    peak = jnp.max(score, axis=0, keepdims=True)
    terms = jnp.exp(score - peak)
    scale = 1.0 / jnp.sum(terms, axis=0, keepdims=True)
    terms = terms.astype(BF16)
    ot = jnp.concatenate(
        [dot(v[h * D : h * D + D], terms[:, h * C : h * C + C]) * scale[:, h * C : h * C + C] for h in range(H)], axis=0
    )
    gated = (g.astype(F32) * ot).astype(BF16)
    stream = cells + dot_tn(gated, wo[...])
    normed = layer_norm(stream).astype(BF16)
    hidden = jnp.maximum(dot(normed, win[...]), 0.0).astype(BF16)
    new = (stream + dot(hidden, wout[...])).astype(BF16).astype(F32)
    for n in range(2):
        for ch in range(2):
            mix[pl.ds(n * 8 + ch * 4 + a, 128, stride=16), :] = new[
                n * 128 : n * 128 + 128, ch * 128 : ch * 128 + 128
            ]
    return dot_nt(wf, layer_norm(new).astype(BF16)).astype(BF16)


def outer_weight(w_ref, block):
    block[...] = jnp.zeros_like(block)
    for c in range(32):
        one = w_ref[c * 32 : c * 32 + 32, :]
        for j in range(4):
            block[c * 128 + j * 32 : c * 128 + j * 32 + 32, j * 128 : j * 128 + 128] = one


def outer_left(a, left_ref, left):
    for n in range(2):
        left[n, a] = left_ref[:, :, a, :, n * 128 : n * 128 + 128].reshape(512, 128).astype(F32)


def outer_right(a, right_ref, right):
    right[a] = right_ref[:, a].reshape(256, 256).T


def outer_products(las, ras, left, right, wide):
    count = 16 * len(las)
    for first in range(0, 32, 8):
        rows = jnp.concatenate(
            [
                jnp.concatenate([left[n, a, pl.ds(c, 16, stride=32), :] for n in range(2)], axis=1)
                for c in range(first, first + 8)
                for a in las
            ],
            axis=0,
        ).astype(BF16)
        for ra in ras:
            product = (dot(rows, right[ra]) * (1.0 / 256)).astype(BF16)
            for c in range(8):
                for half in range(2):
                    at = (first + c) * 128
                    wide[ra * 2 + half, las[0] * 16 : las[0] * 16 + count, at : at + 128] = product[
                        c * count : c * count + count, half * 128 : half * 128 + 128
                    ]


def outer_update(groups, las, wide, block, pairs):
    parts = []
    for (low, high), some in zip(groups, las):
        count = 16 * len(some)
        parts.append(wide[low:high, some[0] * 16 : some[0] * 16 + count, :].reshape((high - low) * count, 4096))
    update = dot(jnp.concatenate(parts, axis=0), block[...])
    at = 0
    for (low, high), some in zip(groups, las):
        for g in range(low, high):
            for a in some:
                for o in range(4):
                    pairs[pl.ds(a * 32 + (g % 2) * 16 + o * 4 + g // 2, 16, stride=128), :] = update[
                        at : at + 16, o * 128 : o * 128 + 128
                    ]
                at += 16


def whole_kernel(
    x_hbm, pair_hbm, bw_hbm, rw_hbm, ro_hbm, cw_hbm, co_hbm, ti_hbm, to_hbm, oi_hbm, oo_hbm,
    ao_hbm, pu_hbm,
    pair, bw, rw, ro, cw, co, ti, to, oi, oo,
    own, xo, bias, qd, kk, vt, gt, mask, mid, mix, wt, sendbuf, cells, fl, fr, lo, ri, left, right, wide, block, pairs,
    ao, pu,
    nsend, nrecv, hrecv, srecv, lrecv, frecv, rrecv, lsem,
    hsend, ssend, xsend, xrecv, csend, crecv, lsend, fsend, rsend,
):
    s, r = lax.axis_index("seq"), lax.axis_index("res")
    here = s * RES + r
    pos = {"x": s // 2, "y": (s % 2) * 2 + r // 8, "z": (r % 8) // 2}
    core = r % 2
    sibling = (s, r + 1 - 2 * core)

    def near(dim, by):
        at = dict(pos)
        at[dim] = (pos[dim] + by) % 4
        return device(at["x"], at["y"], at["z"], core)

    loads = {}
    for k, (name, src, dst) in enumerate(
        (
            ("pair", pair_hbm, pair), ("bw", bw_hbm, bw), ("rw", rw_hbm, rw), ("ro", ro_hbm, ro), ("cw", cw_hbm, cw),
            ("co", co_hbm, co), ("ti", ti_hbm, ti), ("to", to_hbm, to), ("oi", oi_hbm, oi), ("oo", oo_hbm, oo),
            ("keep", x_hbm.at[r], xo.at[r]),
        )
    ):
        loads[name] = pltpu.make_async_copy(src, dst, lsem.at[k])
        loads[name].start()

    def need(name):
        loads.pop(name).wait()

    barrier = pltpu.get_barrier_semaphore()

    def greet(k, carry):
        pl.semaphore_signal(barrier, inc=1, device_id=(s, (r + k) % 16), device_id_type=MESH)
        return carry

    lax.fori_loop(1, 16, greet, 0)
    for dim in "xy":
        for by in (1, 2, 3):
            pl.semaphore_signal(barrier, inc=1, device_id=near(dim, by), device_id_type=MESH)

    need("pair")
    need("bw")
    pair_bias(pair, bw, own)
    mine_at = bias.at[:, 0, pos["y"], pos["z"], core]
    place = pltpu.make_async_copy(own, mine_at, lsem.at[0])
    place.start()
    pl.semaphore_wait(barrier, 21)

    def scatter_x(k, carry):
        other = (r + k) % 16
        remote(x_hbm.at[other], xo.at[r], xsend, xrecv, (s, other)).start()
        return carry

    px, py, pz = pos["x"], pos["y"], pos["z"]
    ALL, MOST, REST = pl.ds(0, 4), pl.ds(0, 3), pl.ds(1, 3)
    LOW, HIGH = pl.ds(0, 2), pl.ds(2, 2)
    HALVES = (LOW, HIGH)
    BY = (1, 3, 2)
    PARTS = [(kind, by) for by in (0, 3, 1, 2) for kind in "yz"]

    def part_of(dx, k, inner=ALL):
        kind, by = PARTS[k]
        if kind == "y":
            return bias.at[LOW, dx, (py + by) % 4, inner, core]
        return bias.at[2, dx, inner, (pz + by) % 4, core]

    def share(group, what):
        remote(what, what, ssend, srecv.at[group], sibling).start()

    def along_x(k):
        for way, by in enumerate((1, 3)):
            remote(part_of(0, k), part_of(4 - by, k), hsend, hrecv.at[k, way], near("x", by)).start()

    def onward_x(*ks):
        for k in ks:
            for way, by in enumerate((1, 3)):
                got = part_of(4 - by, k)
                remote(got, got, hsend, hrecv.at[k, way], near("x", by)).wait_recv()
                remote(
                    part_of(4 - by, k, HALVES[way]), part_of(2, k, HALVES[way]), hsend, hrecv.at[k, 2 + way], near("x", by)
                ).start()
                share(4 - by, got)

    def last_x(*ks):
        for k in ks:
            for way, by in enumerate((1, 3)):
                half = part_of(2, k, HALVES[way])
                remote(half, half, hsend, hrecv.at[k, 2 + way], near("x", by)).wait_recv()
            share(2, part_of(2, k))

    def shared(group):
        half = bias.at[ALL, 0, :, :, 1 - core] if group == 0 else bias.at[MOST, group, :, :, 1 - core]
        if group == 4:
            half = bias.at[3, REST, :, :, 1 - core]
        remote(half, half, hsend, srecv.at[group], sibling).wait_recv()

    copies = []

    def three(dim, src, dst, base):
        made = [remote(src, dst, nsend.at[base + k], nrecv.at[base + k], near(dim, by)) for k, by in enumerate(BY)]
        for copy in made:
            copy.start()
        copies.extend(made)
        return made

    def arrived(made):
        for copy in made:
            copy.wait_recv()

    low_z = three("z", own.at[LOW], bias.at[LOW, 0, py, pz, core], 0)
    high_y = three("y", own.at[HIGH], bias.at[HIGH, 0, py, pz, core], 3)
    t_x = []
    for k, by in enumerate(BY):
        t_x.append(remote(own.at[3], bias.at[3, 4 - by, py, pz, core], nsend.at[6 + k], nrecv.at[6 + k], near("x", by)))
        t_x[k].start()
    copies.extend(t_x)
    lax.fori_loop(1, 16, scatter_x, 0)

    place.wait()
    arrived(low_z)
    mine = bias.at[LOW, 0, py, :, core]
    low_y = three("y", mine, mine, 9)
    along_x(0)
    arrived(high_y)
    mine = bias.at[HIGH, 0, :, pz, core]
    high_z = three("z", mine, mine, 12)
    along_x(1)
    arrived(t_x)
    mine = bias.at[3, REST, py, pz, core]
    t_y = three("y", mine, mine, 15)
    row = lax.broadcasted_iota(jnp.int32, (C, 512), 0) // D
    lane = lax.broadcasted_iota(jnp.int32, (C, 512), 1) // 64
    mask[...] = jnp.where(row == lane, 1.0, 0.0).astype(BF16)
    need("rw")
    for i, at in enumerate((0, 2, 3)):
        wt[0, i * C : i * C + C, :] = rw[:, at * C : at * C + C].T
    for k in range(3):
        low_y[k].wait_recv()
        along_x(2 + 2 * k)
        high_z[k].wait_recv()
        along_x(3 + 2 * k)
        if k == 0:
            onward_x(0, 1)
    share(0, bias.at[:, 0, :, :, core])
    arrived(t_y)
    mine = bias.at[3, REST, :, pz, core]
    t_z = three("z", mine, mine, 18)
    need("keep")
    most = xo.at[pl.ds(0, 15)]
    remote(most, most, xsend, xrecv, sibling).wait()
    row_project(0, xo, wt.at[0], rw[:, C : 2 * C], qd, kk, vt, gt)
    onward_x(2, 3)
    row_project(1, xo, wt.at[0], rw[:, C : 2 * C], qd, kk, vt, gt)
    onward_x(4, 5)
    need("oo")
    outer_weight(oo, block)
    need("cw")
    for i, at in enumerate((0, 2, 3)):
        wt[1, i * C : i * C + C, :] = cw[:, at * C : at * C + C].T
    arrived(t_z)
    share(4, bias.at[3, REST, :, :, core])
    need("ro")

    def attend(q, carry):
        dx = q - q // 2 + 2 * (q % 2) * (1 - q // 2)
        sp = (px + dx) % 4

        @pl.when(q == 0)
        def _():
            shared(0)

        @pl.when(q == 1)
        def _():
            onward_x(6, 7)
            last_x(0, 1)
            shared(4)
            shared(3)

        @pl.when(q == 2)
        def _():
            last_x(2, 3, 4, 5)
            shared(1)

        @pl.when(q == 3)
        def _():
            last_x(6, 7)
            shared(2)

        row_attend(sp, dx, xo, bias, ro, qd, kk, vt, gt, mask, mid, mix)
        rows = mix[pl.ds(pl.multiple_of(sp * 512, 512), 512), :].astype(BF16)
        sendbuf[pl.ds(sp * 32, 32)] = rows.reshape(32, 16, 128)

        for yh in range(2):
            to_s = sp * 2 + yh

            def scatter(i, carry):
                to_r = lax.bitwise_and(r + i, 15)
                other = to_s * 16 + to_r

                @pl.when(other != here)
                def _():
                    remote(sendbuf.at[other], cells.at[here], csend, crecv, (to_s, to_r)).start()

                return carry

            lax.fori_loop(0, 16, scatter, 0, unroll=True)
        return carry

    lax.fori_loop(0, 4, attend, 0)
    cells[here] = sendbuf[here]
    for copy in copies:
        copy.wait_send()
    most = bias.at[:, :, :, :, 0]
    remote(most, most, ssend, srecv.at[0], sibling).wait_send()
    most = bias.at[MOST, MOST, :, :, 0]
    remote(most, most, hsend, srecv.at[0], sibling).wait_send()
    for name in ("co", "ti", "to", "oi"):
        need(name)
    most = cells.at[pl.ds(0, 127)]
    remote(most, most, csend, crecv, sibling).wait()

    mix[...] = cells[...].reshape(2048, 128).astype(F32)
    wf = oi[...]
    column = 2 * s + r // 8
    is_own = column == r
    chip = r // 2

    def onward_left(a):
        most = lo.at[pl.ds(0, 7), core, a]
        remote(most, most, lsend, lrecv.at[a], sibling).wait_recv()
        line = lo.at[:, core, a]
        remote(line, line, fsend, frecv.at[a], sibling).start()

    def residue(a, carry):
        factor = column_step(a, mix, wt.at[1], cw[:, C : 2 * C], co, ti, to, wf)
        fl[a] = factor[:D]
        fr[a] = factor[D:]
        lo[chip, core, a] = factor[:D]

        @pl.when(is_own)
        def _():
            ri[r % 8, a] = factor[D:]

        def send_left(k, carry):
            remote(fl.at[a], lo.at[chip, core, a], lsend, lrecv.at[a], (s, lax.bitwise_and(chip + k, 7) * 2 + core)).start()
            return carry

        def send_right(k, carry):
            @pl.when(jnp.logical_not(jnp.logical_and(is_own, k == 0)))
            def _():
                remote(fr.at[a], ri.at[r % 8, a], rsend, rrecv.at[a], (lax.bitwise_and(s + k, 7), column)).start()

            return carry

        lax.fori_loop(1, 8, send_left, 0, unroll=True)
        lax.fori_loop(0, 8, send_right, 0, unroll=True)

        @pl.when(a > 0)
        def _():
            onward_left(a - 1)

        return carry

    lax.fori_loop(0, 4, residue, 0)
    new = mix[...].astype(BF16).reshape(256, 8, 128)
    for ch in range(2):
        ao[:, :, ch * 128 : ch * 128 + 128] = new[:, ch * 4 : ch * 4 + 4, :]
    save = pltpu.make_async_copy(ao, ao_hbm, lsem.at[0])
    save.start()

    def gathered(a):
        half = lo.at[:, 1 - core, a]
        remote(half, half, fsend, frecv.at[a], sibling).wait_recv()

        @pl.when(is_own)
        def _():
            part = ri.at[pl.ds(0, 7), a]
            remote(part, part, rsend, rrecv.at[a], sibling).wait_recv()

        @pl.when(jnp.logical_not(is_own))
        def _():
            part = ri.at[:, a]
            remote(part, part, rsend, rrecv.at[a], sibling).wait_recv()

        outer_left(a, lo, left)
        outer_right(a, ri, right)

    for a in range(3):
        gathered(a)
    outer_products((0, 1, 2), (0, 1, 2), left, right, wide)
    onward_left(3)
    outer_update(((0, 6),), ((0, 1, 2),), wide, block, pairs)
    gathered(3)
    outer_products((3,), (0, 1, 2, 3), left, right, wide)
    outer_products((0, 1, 2), (3,), left, right, wide)
    outer_update(((0, 8), (6, 8)), ((3,), (0, 1, 2)), wide, block, pairs)
    pu[...] = pairs[...].astype(BF16)
    most = lo.at[pl.ds(0, 7), core]
    remote(most, most, lsend, lrecv.at[0], sibling).wait_send()
    half = lo.at[:, 1 - core]
    remote(half, half, fsend, lrecv.at[0], sibling).wait_send()

    @pl.when(is_own)
    def _():
        part = ri.at[pl.ds(0, 7)]
        remote(part, part, rsend, lrecv.at[0], sibling).wait_send()

    @pl.when(jnp.logical_not(is_own))
    def _():
        remote(ri, ri, rsend, lrecv.at[0], sibling).wait_send()

    last = pltpu.make_async_copy(pu, pu_hbm, lsem.at[1])
    last.start()
    last.wait()
    save.wait()


def body(
    alignment,
    pair_state,
    bias_weight,
    row_weight,
    row_output_weight,
    column_weight,
    column_output_weight,
    transition_in,
    transition_out,
    outer_in,
    outer_out,
):
    dma = pltpu.SemaphoreType.DMA
    new, update = pl.pallas_call(
        whole_kernel,
        out_shape=(jax.ShapeDtypeStruct((256, 4, C), BF16), jax.ShapeDtypeStruct((2048, 128), BF16)),
        in_specs=[ANY] * 11,
        out_specs=(ANY, ANY),
        scratch_shapes=[
            pltpu.VMEM((64, 32, 128), BF16),
            pltpu.VMEM((8, 128), BF16),
            pltpu.VMEM((C, 4 * C), BF16),
            pltpu.VMEM((C, C), BF16),
            pltpu.VMEM((C, 4 * C), BF16),
            pltpu.VMEM((C, C), BF16),
            pltpu.VMEM((C, 4 * C), BF16),
            pltpu.VMEM((4 * C, C), BF16),
            pltpu.VMEM((64, C), BF16),
            pltpu.VMEM((1024, 128), BF16),
            pltpu.VMEM((4, 32, 128), BF16),
            pltpu.VMEM((16, 2, 32, C), BF16),
            pltpu.VMEM((4, 4, 4, 4, 2, 32, 128), BF16),
            pltpu.VMEM((2, 8, C, 128), BF16),
            pltpu.VMEM((2, 512, C), BF16),
            pltpu.VMEM((2, C, 512), BF16),
            pltpu.VMEM((2, 4, C, 128), BF16),
            pltpu.VMEM((C, 512), BF16),
            pltpu.VMEM((2, 2, 128, 128), F32),
            pltpu.VMEM((2048, 128), F32),
            pltpu.VMEM((2, 3 * C, C), BF16),
            pltpu.VMEM((128, 16, 128), BF16),
            pltpu.VMEM((128, 16, 128), BF16),
            pltpu.VMEM((4, D, 256), BF16),
            pltpu.VMEM((4, D, 256), BF16),
            pltpu.VMEM((8, 2, 4, D, 256), BF16),
            pltpu.VMEM((8, 4, D, 256), BF16),
            pltpu.VMEM((2, 4, 512, 128), F32),
            pltpu.VMEM((4, 256, 256), BF16),
            pltpu.VMEM((8, 64, 4096), BF16),
            pltpu.VMEM((4096, 512), BF16),
            pltpu.VMEM((2048, 128), F32),
            pltpu.VMEM((256, 4, C), BF16),
            pltpu.VMEM((2048, 128), BF16),
            dma((21,)),
            dma((21,)),
            dma((8, 4)),
            dma((5,)),
            dma((4,)),
            dma((4,)),
            dma((4,)),
            dma((11,)),
        ]
        + [dma] * 9,
        compiler_params=pltpu.CompilerParams(collective_id=0, has_side_effects=True, vmem_limit_bytes=56 << 20),
        name="evoformer",
    )(
        alignment.reshape(16, 2, 32, C),
        pair_state,
        bias_weight.T,
        row_weight,
        row_output_weight,
        column_weight,
        column_output_weight,
        transition_in,
        transition_out,
        outer_in.T,
        outer_out,
    )
    pair_update = update.reshape(64, 32, 128)
    return (new, pair_update)


def solution(mesh):
    in_specs = (P("seq", "res", None), P("seq", "res", None)) + (P(),) * 9
    out_specs = (P(None, ("seq", "res"), None), P("seq", "res", None))
    return jax.shard_map(body, mesh=mesh, in_specs=in_specs, out_specs=out_specs, check_vma=False)
```

```python
import functools

import jax
import jax.numpy as jnp
from jax import lax
from jax.experimental import pallas as pl
from jax.experimental.pallas import tpu as pltpu
from jax.sharding import PartitionSpec as P

H = 8
D = 32
C = 256
SEQ = 8
RES = 16
EPS = 1e-05
MESH = pl.DeviceIdType.MESH
F32 = jnp.float32
BF16 = jnp.bfloat16
ANY = pl.BlockSpec(memory_space=pl.ANY)
VMEM = pl.BlockSpec(memory_space=pltpu.VMEM)
NT = (((1,), (1,)), ((), ()))
TN = (((0,), (0,)), ((), ()))


def layer_norm(values):
    center = values - jnp.mean(values, axis=-1, keepdims=True)
    spread = jnp.mean(center * center, axis=-1, keepdims=True)
    return center * lax.rsqrt(spread + EPS)


def dot(a, b):
    return jnp.dot(a, b, preferred_element_type=F32)


def dot_nt(a, b):
    return lax.dot_general(a, b, NT, preferred_element_type=F32)


def dot_tn(a, b):
    return lax.dot_general(a, b, TN, preferred_element_type=F32)


def project(x, wt, wk):
    proj = dot_nt(wt, x)
    q = (proj[:C] * D ** (-0.5)).astype(BF16)
    v = proj[C : 2 * C].astype(BF16)
    g = jax.nn.sigmoid(proj[2 * C :]).astype(BF16)
    k = dot(x, wk).astype(BF16)
    return q, k, v, g


def device(x, y, z, core):
    return (x * 2 + y // 2, (y % 2) * 8 + z * 2 + core)


def remote(src, dst, send, recv, target):
    return pltpu.make_async_remote_copy(
        src_ref=src, dst_ref=dst, send_sem=send, recv_sem=recv, device_id=target, device_id_type=MESH
    )


def pair_bias(pair_ref, weight_ref, out_ref):
    lane = lax.broadcasted_iota(jnp.int32, (32, 512), 1) % 64
    narrow = weight_ref[...].astype(F32)
    weight = jnp.concatenate([jnp.broadcast_to(narrow[h : h + 1], (64, 128)) for h in range(8)], axis=0).astype(BF16)
    total = jnp.zeros((32, 512), F32)
    for k in range(8):
        rows = pair_ref[k * 8 : k * 8 + 8].reshape(256, 128).astype(F32)
        spread = dot_nt(layer_norm(rows).astype(BF16), weight)
        for one in range(8):
            total = jnp.where(lane == k * 8 + one, spread[one * 32 : one * 32 + 32], total)
    total = total.astype(BF16)
    for t in range(4):
        out_ref[t] = total[:, t * 128 : t * 128 + 128]


def row_project(n, x_ref, wt, wk, qd, kk, vt, gt):
    low = lax.broadcasted_iota(jnp.int32, (C, 128), 1) < 64
    x = x_ref[:, n].reshape(512, C).astype(F32)
    q, k, v, g = project(layer_norm(x).astype(BF16), wt[...], wk)
    kk[n] = k
    vt[n] = v
    for t in range(4):
        gt[n, t] = g[:, t * 128 : t * 128 + 128]
        tile = q[:, t * 128 : t * 128 + 128].astype(F32)
        other = pltpu.roll(tile, 64, axis=1)
        qd[n, 2 * t] = jnp.where(low, tile, other).astype(BF16)
        qd[n, 2 * t + 1] = jnp.where(low, other, tile).astype(BF16)


def row_attend(sp, dx, x_ref, bias_ref, wo, qd, kk, vt, gt, mask, mid, mix):
    low = lax.broadcasted_iota(jnp.int32, (D, 128), 1) < 64
    bias = jnp.concatenate(
        [bias_ref[t, dx, 2 * e : 2 * e + 2].reshape(512, 128) for e in range(2) for t in range(4)], axis=1
    ).astype(F32)
    gated, cells = [], []
    for n in range(2):
        wide = jnp.concatenate([jnp.concatenate([qd[n, sp * 2 + e]] * 4, axis=1) * mask[...] for e in range(2)], axis=1)
        score = dot(kk[n], wide) + bias
        peak = jnp.max(score, axis=0, keepdims=True)
        terms = jnp.exp(score - peak)
        scale = 1.0 / jnp.sum(terms, axis=0, keepdims=True)
        terms = terms.astype(BF16)
        halves = []
        for e in range(2):
            parts = []
            for half in range(2):
                at = e * 512 + half * 256
                o = dot(vt[n, half * 128 : half * 128 + 128, :], terms[:, at : at + 256]) * scale[:, at : at + 256]
                for h in range(4):
                    part = o[h * D : h * D + D, (h // 2) * 128 : (h // 2) * 128 + 128]
                    if h % 2 != e:
                        part = pltpu.roll(part, 64, axis=1)
                    parts.append(part)
            halves.append(parts)
        ot = jnp.concatenate([jnp.where(low, a, b) for a, b in zip(*halves)], axis=0)
        gated.append((gt[n, sp].astype(F32) * ot).astype(BF16))
        cells.append(x_ref[pl.ds(sp * 4, 4), n].reshape(128, C).astype(F32))
    new = jnp.concatenate(cells, axis=0) + dot_tn(jnp.concatenate(gated, axis=1), wo[...])
    for n in range(2):
        for ch in range(2):
            mid[n, ch] = new[n * 128 : n * 128 + 128, ch * 128 : ch * 128 + 128]
    for n in range(2):
        for ch in range(2):
            for a in range(4):
                mix[pl.ds(sp * 512 + n * 8 + ch * 4 + a, 32, stride=16), :] = mid[n, ch, pl.ds(a, 32, stride=4), :]


def column_step(a, mix, wt, wk, wo, win, wout, wf):
    head = lax.broadcasted_iota(jnp.int32, (C, C), 0) // D
    cells = jnp.concatenate(
        [
            jnp.concatenate([mix[pl.ds(n * 8 + ch * 4 + a, 128, stride=16), :] for ch in range(2)], axis=1)
            for n in range(2)
        ],
        axis=0,
    )
    q, k, v, g = project(layer_norm(cells).astype(BF16), wt[...], wk)
    wide = jnp.concatenate([jnp.where(head == h, q, jnp.zeros_like(q)) for h in range(H)], axis=1)
    score = dot(k, wide)
    peak = jnp.max(score, axis=0, keepdims=True)
    terms = jnp.exp(score - peak)
    scale = 1.0 / jnp.sum(terms, axis=0, keepdims=True)
    terms = terms.astype(BF16)
    ot = jnp.concatenate(
        [dot(v[h * D : h * D + D], terms[:, h * C : h * C + C]) * scale[:, h * C : h * C + C] for h in range(H)], axis=0
    )
    gated = (g.astype(F32) * ot).astype(BF16)
    stream = cells + dot_tn(gated, wo[...])
    normed = layer_norm(stream).astype(BF16)
    hidden = jnp.maximum(dot(normed, win[...]), 0.0).astype(BF16)
    new = (stream + dot(hidden, wout[...])).astype(BF16).astype(F32)
    for n in range(2):
        for ch in range(2):
            mix[pl.ds(n * 8 + ch * 4 + a, 128, stride=16), :] = new[
                n * 128 : n * 128 + 128, ch * 128 : ch * 128 + 128
            ]
    return dot_nt(wf, layer_norm(new).astype(BF16)).astype(BF16)


def outer_weight(w_ref, block):
    block[...] = jnp.zeros_like(block)
    for c in range(32):
        one = w_ref[c * 32 : c * 32 + 32, :]
        for j in range(4):
            block[c * 128 + j * 32 : c * 128 + j * 32 + 32, j * 128 : j * 128 + 128] = one


def outer_left(a, left_ref, left):
    for n in range(2):
        left[n, a] = left_ref[:, :, a, :, n * 128 : n * 128 + 128].reshape(512, 128).astype(F32)


def outer_right(a, right_ref, right):
    right[a] = right_ref[:, a].reshape(256, 256).T


def outer_products(las, ras, left, right, wide):
    count = 16 * len(las)
    for first in range(0, 32, 8):
        rows = jnp.concatenate(
            [
                jnp.concatenate([left[n, a, pl.ds(c, 16, stride=32), :] for n in range(2)], axis=1)
                for c in range(first, first + 8)
                for a in las
            ],
            axis=0,
        ).astype(BF16)
        for ra in ras:
            product = (dot(rows, right[ra]) * (1.0 / 256)).astype(BF16)
            for c in range(8):
                for half in range(2):
                    at = (first + c) * 128
                    wide[ra * 2 + half, las[0] * 16 : las[0] * 16 + count, at : at + 128] = product[
                        c * count : c * count + count, half * 128 : half * 128 + 128
                    ]


def outer_update(groups, las, wide, block, pairs):
    parts = []
    for (low, high), some in zip(groups, las):
        count = 16 * len(some)
        parts.append(wide[low:high, some[0] * 16 : some[0] * 16 + count, :].reshape((high - low) * count, 4096))
    update = dot(jnp.concatenate(parts, axis=0), block[...])
    at = 0
    for (low, high), some in zip(groups, las):
        for g in range(low, high):
            for a in some:
                for o in range(4):
                    pairs[pl.ds(a * 32 + (g % 2) * 16 + o * 4 + g // 2, 16, stride=128), :] = update[
                        at : at + 16, o * 128 : o * 128 + 128
                    ]
                at += 16


def whole_kernel(
    x_hbm, pair_hbm, bw_hbm, rw_hbm, ro_hbm, cw_hbm, co_hbm, ti_hbm, to_hbm, oi_hbm, oo_hbm,
    ao_hbm, pu_hbm,
    pair, bw, rw, ro, cw, co, ti, to, oi, oo,
    own, xo, bias, qd, kk, vt, gt, mask, mid, mix, wt, sendbuf, cells, fl, fr, lo, ri, left, right, wide, block, pairs,
    ao, pu,
    nsend, nrecv, hrecv, srecv, lrecv, frecv, rrecv, lsem,
    hsend, ssend, xsend, xrecv, csend, crecv, lsend, fsend, rsend,
):
    s, r = lax.axis_index("seq"), lax.axis_index("res")
    here = s * RES + r
    pos = {"x": s // 2, "y": (s % 2) * 2 + r // 8, "z": (r % 8) // 2}
    core = r % 2
    sibling = (s, r + 1 - 2 * core)

    def near(dim, by):
        at = dict(pos)
        at[dim] = (pos[dim] + by) % 4
        return device(at["x"], at["y"], at["z"], core)

    loads = {}
    for k, (name, src, dst) in enumerate(
        (
            ("pair", pair_hbm, pair), ("bw", bw_hbm, bw), ("rw", rw_hbm, rw), ("ro", ro_hbm, ro), ("cw", cw_hbm, cw),
            ("co", co_hbm, co), ("ti", ti_hbm, ti), ("to", to_hbm, to), ("oi", oi_hbm, oi), ("oo", oo_hbm, oo),
            ("keep", x_hbm.at[r], xo.at[r]),
        )
    ):
        loads[name] = pltpu.make_async_copy(src, dst, lsem.at[k])
        loads[name].start()

    def need(name):
        loads.pop(name).wait()

    barrier = pltpu.get_barrier_semaphore()

    def greet(k, carry):
        pl.semaphore_signal(barrier, inc=1, device_id=(s, (r + k) % 16), device_id_type=MESH)
        return carry

    lax.fori_loop(1, 16, greet, 0)
    for dim in "xy":
        for by in (1, 2, 3):
            pl.semaphore_signal(barrier, inc=1, device_id=near(dim, by), device_id_type=MESH)

    need("pair")
    need("bw")
    pair_bias(pair, bw, own)
    mine_at = bias.at[:, 0, pos["y"], pos["z"], core]
    place = pltpu.make_async_copy(own, mine_at, lsem.at[0])
    place.start()
    pl.semaphore_wait(barrier, 21)

    def scatter_x(k, carry):
        other = (r + k) % 16
        remote(x_hbm.at[other], xo.at[r], xsend, xrecv, (s, other)).start()
        return carry

    px, py, pz = pos["x"], pos["y"], pos["z"]
    ALL, MOST, REST = pl.ds(0, 4), pl.ds(0, 3), pl.ds(1, 3)
    LOW, HIGH = pl.ds(0, 2), pl.ds(2, 2)
    HALVES = (LOW, HIGH)
    BY = (1, 3, 2)
    PARTS = [(kind, by) for by in (0, 3, 1, 2) for kind in "yz"]

    def part_of(dx, k, inner=ALL):
        kind, by = PARTS[k]
        if kind == "y":
            return bias.at[LOW, dx, (py + by) % 4, inner, core]
        return bias.at[2, dx, inner, (pz + by) % 4, core]

    def share(group, what):
        remote(what, what, ssend, srecv.at[group], sibling).start()

    def along_x(k):
        for way, by in enumerate((1, 3)):
            remote(part_of(0, k), part_of(4 - by, k), hsend, hrecv.at[k, way], near("x", by)).start()

    def onward_x(*ks):
        for k in ks:
            for way, by in enumerate((1, 3)):
                got = part_of(4 - by, k)
                remote(got, got, hsend, hrecv.at[k, way], near("x", by)).wait_recv()
                remote(
                    part_of(4 - by, k, HALVES[way]), part_of(2, k, HALVES[way]), hsend, hrecv.at[k, 2 + way], near("x", by)
                ).start()
                share(4 - by, got)

    def last_x(*ks):
        for k in ks:
            for way, by in enumerate((1, 3)):
                half = part_of(2, k, HALVES[way])
                remote(half, half, hsend, hrecv.at[k, 2 + way], near("x", by)).wait_recv()
            share(2, part_of(2, k))

    def shared(group):
        half = bias.at[ALL, 0, :, :, 1 - core] if group == 0 else bias.at[MOST, group, :, :, 1 - core]
        if group == 4:
            half = bias.at[3, REST, :, :, 1 - core]
        remote(half, half, hsend, srecv.at[group], sibling).wait_recv()

    copies = []

    def three(dim, src, dst, base):
        made = [remote(src, dst, nsend.at[base + k], nrecv.at[base + k], near(dim, by)) for k, by in enumerate(BY)]
        for copy in made:
            copy.start()
        copies.extend(made)
        return made

    def arrived(made):
        for copy in made:
            copy.wait_recv()

    low_z = three("z", own.at[LOW], bias.at[LOW, 0, py, pz, core], 0)
    high_y = three("y", own.at[HIGH], bias.at[HIGH, 0, py, pz, core], 3)
    t_x = []
    for k, by in enumerate(BY):
        t_x.append(remote(own.at[3], bias.at[3, 4 - by, py, pz, core], nsend.at[6 + k], nrecv.at[6 + k], near("x", by)))
        t_x[k].start()
    copies.extend(t_x)
    lax.fori_loop(1, 16, scatter_x, 0)

    place.wait()
    arrived(low_z)
    mine = bias.at[LOW, 0, py, :, core]
    low_y = three("y", mine, mine, 9)
    along_x(0)
    arrived(high_y)
    mine = bias.at[HIGH, 0, :, pz, core]
    high_z = three("z", mine, mine, 12)
    along_x(1)
    arrived(t_x)
    mine = bias.at[3, REST, py, pz, core]
    t_y = three("y", mine, mine, 15)
    row = lax.broadcasted_iota(jnp.int32, (C, 512), 0) // D
    lane = lax.broadcasted_iota(jnp.int32, (C, 512), 1) // 64
    mask[...] = jnp.where(row == lane, 1.0, 0.0).astype(BF16)
    need("rw")
    for i, at in enumerate((0, 2, 3)):
        wt[0, i * C : i * C + C, :] = rw[:, at * C : at * C + C].T
    for k in range(3):
        low_y[k].wait_recv()
        along_x(2 + 2 * k)
        high_z[k].wait_recv()
        along_x(3 + 2 * k)
        if k == 0:
            onward_x(0, 1)
    share(0, bias.at[:, 0, :, :, core])
    arrived(t_y)
    mine = bias.at[3, REST, :, pz, core]
    t_z = three("z", mine, mine, 18)
    need("keep")
    most = xo.at[pl.ds(0, 15)]
    remote(most, most, xsend, xrecv, sibling).wait()
    row_project(0, xo, wt.at[0], rw[:, C : 2 * C], qd, kk, vt, gt)
    onward_x(2, 3)
    row_project(1, xo, wt.at[0], rw[:, C : 2 * C], qd, kk, vt, gt)
    onward_x(4, 5)
    need("oo")
    outer_weight(oo, block)
    need("cw")
    for i, at in enumerate((0, 2, 3)):
        wt[1, i * C : i * C + C, :] = cw[:, at * C : at * C + C].T
    arrived(t_z)
    share(4, bias.at[3, REST, :, :, core])
    need("ro")

    def attend(q, carry):
        dx = q - q // 2 + 2 * (q % 2) * (1 - q // 2)
        sp = (px + dx) % 4

        @pl.when(q == 0)
        def _():
            shared(0)

        @pl.when(q == 1)
        def _():
            onward_x(6, 7)
            last_x(0, 1)
            shared(4)
            shared(3)

        @pl.when(q == 2)
        def _():
            last_x(2, 3, 4, 5)
            shared(1)

        @pl.when(q == 3)
        def _():
            last_x(6, 7)
            shared(2)

        row_attend(sp, dx, xo, bias, ro, qd, kk, vt, gt, mask, mid, mix)
        rows = mix[pl.ds(pl.multiple_of(sp * 512, 512), 512), :].astype(BF16)
        sendbuf[pl.ds(sp * 32, 32)] = rows.reshape(32, 16, 128)

        for yh in range(2):
            to_s = sp * 2 + yh

            def scatter(i, carry):
                to_r = lax.bitwise_and(r + i, 15)
                other = to_s * 16 + to_r

                @pl.when(other != here)
                def _():
                    remote(sendbuf.at[other], cells.at[here], csend, crecv, (to_s, to_r)).start()

                return carry

            lax.fori_loop(0, 16, scatter, 0, unroll=True)
        return carry

    lax.fori_loop(0, 4, attend, 0, unroll=True)
    cells[here] = sendbuf[here]
    for copy in copies:
        copy.wait_send()
    most = bias.at[:, :, :, :, 0]
    remote(most, most, ssend, srecv.at[0], sibling).wait_send()
    most = bias.at[MOST, MOST, :, :, 0]
    remote(most, most, hsend, srecv.at[0], sibling).wait_send()
    for name in ("co", "ti", "to", "oi"):
        need(name)
    most = cells.at[pl.ds(0, 127)]
    remote(most, most, csend, crecv, sibling).wait()

    mix[...] = cells[...].reshape(2048, 128).astype(F32)
    wf = oi[...]
    column = 2 * s + r // 8
    is_own = column == r
    chip = r // 2

    def onward_left(a):
        most = lo.at[pl.ds(0, 7), core, a]
        remote(most, most, lsend, lrecv.at[a], sibling).wait_recv()
        line = lo.at[:, core, a]
        remote(line, line, fsend, frecv.at[a], sibling).start()

    def residue(a, carry):
        factor = column_step(a, mix, wt.at[1], cw[:, C : 2 * C], co, ti, to, wf)
        fl[a] = factor[:D]
        fr[a] = factor[D:]
        lo[chip, core, a] = factor[:D]

        @pl.when(is_own)
        def _():
            ri[r % 8, a] = factor[D:]

        def send_left(k, carry):
            remote(fl.at[a], lo.at[chip, core, a], lsend, lrecv.at[a], (s, lax.bitwise_and(chip + k, 7) * 2 + core)).start()
            return carry

        def send_right(k, carry):
            @pl.when(jnp.logical_not(jnp.logical_and(is_own, k == 0)))
            def _():
                remote(fr.at[a], ri.at[r % 8, a], rsend, rrecv.at[a], (lax.bitwise_and(s + k, 7), column)).start()

            return carry

        lax.fori_loop(1, 8, send_left, 0, unroll=True)
        lax.fori_loop(0, 8, send_right, 0, unroll=True)

        @pl.when(a > 0)
        def _():
            onward_left(a - 1)

        return carry

    lax.fori_loop(0, 4, residue, 0)
    new = mix[...].astype(BF16).reshape(256, 8, 128)
    for ch in range(2):
        ao[:, :, ch * 128 : ch * 128 + 128] = new[:, ch * 4 : ch * 4 + 4, :]
    save = pltpu.make_async_copy(ao, ao_hbm, lsem.at[0])
    save.start()

    def gathered(a):
        half = lo.at[:, 1 - core, a]
        remote(half, half, fsend, frecv.at[a], sibling).wait_recv()

        @pl.when(is_own)
        def _():
            part = ri.at[pl.ds(0, 7), a]
            remote(part, part, rsend, rrecv.at[a], sibling).wait_recv()

        @pl.when(jnp.logical_not(is_own))
        def _():
            part = ri.at[:, a]
            remote(part, part, rsend, rrecv.at[a], sibling).wait_recv()

        outer_left(a, lo, left)
        outer_right(a, ri, right)

    for a in range(3):
        gathered(a)
    outer_products((0, 1, 2), (0, 1, 2), left, right, wide)
    onward_left(3)
    outer_update(((0, 6),), ((0, 1, 2),), wide, block, pairs)
    gathered(3)
    outer_products((3,), (0, 1, 2, 3), left, right, wide)
    outer_products((0, 1, 2), (3,), left, right, wide)
    outer_update(((0, 8), (6, 8)), ((3,), (0, 1, 2)), wide, block, pairs)
    pu[...] = pairs[...].astype(BF16)
    most = lo.at[pl.ds(0, 7), core]
    remote(most, most, lsend, lrecv.at[0], sibling).wait_send()
    half = lo.at[:, 1 - core]
    remote(half, half, fsend, lrecv.at[0], sibling).wait_send()

    @pl.when(is_own)
    def _():
        part = ri.at[pl.ds(0, 7)]
        remote(part, part, rsend, lrecv.at[0], sibling).wait_send()

    @pl.when(jnp.logical_not(is_own))
    def _():
        remote(ri, ri, rsend, lrecv.at[0], sibling).wait_send()

    last = pltpu.make_async_copy(pu, pu_hbm, lsem.at[1])
    last.start()
    last.wait()
    save.wait()


def body(
    alignment,
    pair_state,
    bias_weight,
    row_weight,
    row_output_weight,
    column_weight,
    column_output_weight,
    transition_in,
    transition_out,
    outer_in,
    outer_out,
):
    dma = pltpu.SemaphoreType.DMA
    new, update = pl.pallas_call(
        whole_kernel,
        out_shape=(jax.ShapeDtypeStruct((256, 4, C), BF16), jax.ShapeDtypeStruct((2048, 128), BF16)),
        in_specs=[ANY] * 11,
        out_specs=(ANY, ANY),
        scratch_shapes=[
            pltpu.VMEM((64, 32, 128), BF16),
            pltpu.VMEM((8, 128), BF16),
            pltpu.VMEM((C, 4 * C), BF16),
            pltpu.VMEM((C, C), BF16),
            pltpu.VMEM((C, 4 * C), BF16),
            pltpu.VMEM((C, C), BF16),
            pltpu.VMEM((C, 4 * C), BF16),
            pltpu.VMEM((4 * C, C), BF16),
            pltpu.VMEM((64, C), BF16),
            pltpu.VMEM((1024, 128), BF16),
            pltpu.VMEM((4, 32, 128), BF16),
            pltpu.VMEM((16, 2, 32, C), BF16),
            pltpu.VMEM((4, 4, 4, 4, 2, 32, 128), BF16),
            pltpu.VMEM((2, 8, C, 128), BF16),
            pltpu.VMEM((2, 512, C), BF16),
            pltpu.VMEM((2, C, 512), BF16),
            pltpu.VMEM((2, 4, C, 128), BF16),
            pltpu.VMEM((C, 512), BF16),
            pltpu.VMEM((2, 2, 128, 128), F32),
            pltpu.VMEM((2048, 128), F32),
            pltpu.VMEM((2, 3 * C, C), BF16),
            pltpu.VMEM((128, 16, 128), BF16),
            pltpu.VMEM((128, 16, 128), BF16),
            pltpu.VMEM((4, D, 256), BF16),
            pltpu.VMEM((4, D, 256), BF16),
            pltpu.VMEM((8, 2, 4, D, 256), BF16),
            pltpu.VMEM((8, 4, D, 256), BF16),
            pltpu.VMEM((2, 4, 512, 128), F32),
            pltpu.VMEM((4, 256, 256), BF16),
            pltpu.VMEM((8, 64, 4096), BF16),
            pltpu.VMEM((4096, 512), BF16),
            pltpu.VMEM((2048, 128), F32),
            pltpu.VMEM((256, 4, C), BF16),
            pltpu.VMEM((2048, 128), BF16),
            dma((21,)),
            dma((21,)),
            dma((8, 4)),
            dma((5,)),
            dma((4,)),
            dma((4,)),
            dma((4,)),
            dma((11,)),
        ]
        + [dma] * 9,
        compiler_params=pltpu.CompilerParams(collective_id=0, has_side_effects=True, vmem_limit_bytes=56 << 20),
        name="evoformer",
    )(
        alignment.reshape(16, 2, 32, C),
        pair_state,
        bias_weight.T,
        row_weight,
        row_output_weight,
        column_weight,
        column_output_weight,
        transition_in,
        transition_out,
        outer_in.T,
        outer_out,
    )
    pair_update = update.reshape(64, 32, 128)
    return (new, pair_update)


def solution(mesh):
    in_specs = (P("seq", "res", None), P("seq", "res", None)) + (P(),) * 9
    out_specs = (P(None, ("seq", "res"), None), P("seq", "res", None))
    return jax.shard_map(body, mesh=mesh, in_specs=in_specs, out_specs=out_specs, check_vma=False)
```

```python
import functools

import jax
import jax.numpy as jnp
from jax import lax
from jax.experimental import pallas as pl
from jax.experimental.pallas import tpu as pltpu
from jax.sharding import PartitionSpec as P

H = 8
D = 32
C = 256
SEQ = 8
RES = 16
EPS = 1e-05
MESH = pl.DeviceIdType.MESH
F32 = jnp.float32
BF16 = jnp.bfloat16
ANY = pl.BlockSpec(memory_space=pl.ANY)
VMEM = pl.BlockSpec(memory_space=pltpu.VMEM)
NT = (((1,), (1,)), ((), ()))
TN = (((0,), (0,)), ((), ()))


def layer_norm(values):
    center = values - jnp.mean(values, axis=-1, keepdims=True)
    spread = jnp.mean(center * center, axis=-1, keepdims=True)
    return center * lax.rsqrt(spread + EPS)


def dot(a, b):
    return jnp.dot(a, b, preferred_element_type=F32)


def dot_nt(a, b):
    return lax.dot_general(a, b, NT, preferred_element_type=F32)


def dot_tn(a, b):
    return lax.dot_general(a, b, TN, preferred_element_type=F32)


def project(x, wt, wk):
    proj = dot_nt(wt, x)
    q = (proj[:C] * D ** (-0.5)).astype(BF16)
    v = proj[C : 2 * C].astype(BF16)
    g = jax.nn.sigmoid(proj[2 * C :]).astype(BF16)
    k = dot(x, wk).astype(BF16)
    return q, k, v, g


def device(x, y, z, core):
    return (x * 2 + y // 2, (y % 2) * 8 + z * 2 + core)


def remote(src, dst, send, recv, target):
    return pltpu.make_async_remote_copy(
        src_ref=src, dst_ref=dst, send_sem=send, recv_sem=recv, device_id=target, device_id_type=MESH
    )


def pair_bias(pair_ref, weight_ref, out_ref):
    lane = lax.broadcasted_iota(jnp.int32, (32, 512), 1) % 64
    narrow = weight_ref[...].astype(F32)
    weight = jnp.concatenate([jnp.broadcast_to(narrow[h : h + 1], (64, 128)) for h in range(8)], axis=0).astype(BF16)
    total = jnp.zeros((32, 512), F32)
    for k in range(8):
        rows = pair_ref[k * 8 : k * 8 + 8].reshape(256, 128).astype(F32)
        spread = dot_nt(layer_norm(rows).astype(BF16), weight)
        for one in range(8):
            total = jnp.where(lane == k * 8 + one, spread[one * 32 : one * 32 + 32], total)
    total = total.astype(BF16)
    for t in range(4):
        out_ref[t] = total[:, t * 128 : t * 128 + 128]


def row_project(n, x_ref, wt, wk, qd, kk, vt, gt):
    low = lax.broadcasted_iota(jnp.int32, (C, 128), 1) < 64
    x = x_ref[:, n].reshape(512, C).astype(F32)
    q, k, v, g = project(layer_norm(x).astype(BF16), wt[...], wk)
    kk[n] = k
    vt[n] = v
    for t in range(4):
        gt[n, t] = g[:, t * 128 : t * 128 + 128]
        tile = q[:, t * 128 : t * 128 + 128].astype(F32)
        other = pltpu.roll(tile, 64, axis=1)
        qd[n, 2 * t] = jnp.where(low, tile, other).astype(BF16)
        qd[n, 2 * t + 1] = jnp.where(low, other, tile).astype(BF16)


def row_attend(sp, dx, x_ref, bias_ref, wo, qd, kk, vt, gt, mask, mid, mix):
    low = lax.broadcasted_iota(jnp.int32, (D, 128), 1) < 64
    bias = jnp.concatenate(
        [bias_ref[t, dx, 2 * e : 2 * e + 2].reshape(512, 128) for e in range(2) for t in range(4)], axis=1
    ).astype(F32)
    gated, cells = [], []
    for n in range(2):
        wide = jnp.concatenate([jnp.concatenate([qd[n, sp * 2 + e]] * 4, axis=1) * mask[...] for e in range(2)], axis=1)
        score = dot(kk[n], wide) + bias
        peak = jnp.max(score, axis=0, keepdims=True)
        terms = jnp.exp(score - peak)
        scale = 1.0 / jnp.sum(terms, axis=0, keepdims=True)
        terms = terms.astype(BF16)
        halves = []
        for e in range(2):
            parts = []
            for half in range(2):
                at = e * 512 + half * 256
                o = dot(vt[n, half * 128 : half * 128 + 128, :], terms[:, at : at + 256]) * scale[:, at : at + 256]
                for h in range(4):
                    part = o[h * D : h * D + D, (h // 2) * 128 : (h // 2) * 128 + 128]
                    if h % 2 != e:
                        part = pltpu.roll(part, 64, axis=1)
                    parts.append(part)
            halves.append(parts)
        ot = jnp.concatenate([jnp.where(low, a, b) for a, b in zip(*halves)], axis=0)
        gated.append((gt[n, sp].astype(F32) * ot).astype(BF16))
        cells.append(x_ref[pl.ds(sp * 4, 4), n].reshape(128, C).astype(F32))
    new = jnp.concatenate(cells, axis=0) + dot_tn(jnp.concatenate(gated, axis=1), wo[...])
    for n in range(2):
        for ch in range(2):
            mid[n, ch] = new[n * 128 : n * 128 + 128, ch * 128 : ch * 128 + 128]
    for n in range(2):
        for ch in range(2):
            for a in range(4):
                mix[pl.ds(sp * 512 + n * 8 + ch * 4 + a, 32, stride=16), :] = mid[n, ch, pl.ds(a, 32, stride=4), :]


def column_step(a, mix, wt, wk, wo, win, wout, wf):
    head = lax.broadcasted_iota(jnp.int32, (C, C), 0) // D
    cells = jnp.concatenate(
        [
            jnp.concatenate([mix[pl.ds(n * 8 + ch * 4 + a, 128, stride=16), :] for ch in range(2)], axis=1)
            for n in range(2)
        ],
        axis=0,
    )
    q, k, v, g = project(layer_norm(cells).astype(BF16), wt[...], wk)
    wide = jnp.concatenate([jnp.where(head == h, q, jnp.zeros_like(q)) for h in range(H)], axis=1)
    score = dot(k, wide)
    peak = jnp.max(score, axis=0, keepdims=True)
    terms = jnp.exp(score - peak)
    scale = 1.0 / jnp.sum(terms, axis=0, keepdims=True)
    terms = terms.astype(BF16)
    ot = jnp.concatenate(
        [dot(v[h * D : h * D + D], terms[:, h * C : h * C + C]) * scale[:, h * C : h * C + C] for h in range(H)], axis=0
    )
    gated = (g.astype(F32) * ot).astype(BF16)
    stream = cells + dot_tn(gated, wo[...])
    normed = layer_norm(stream).astype(BF16)
    hidden = jnp.maximum(dot(normed, win[...]), 0.0).astype(BF16)
    new = (stream + dot(hidden, wout[...])).astype(BF16).astype(F32)
    for n in range(2):
        for ch in range(2):
            mix[pl.ds(n * 8 + ch * 4 + a, 128, stride=16), :] = new[
                n * 128 : n * 128 + 128, ch * 128 : ch * 128 + 128
            ]
    return dot_nt(wf, layer_norm(new).astype(BF16)).astype(BF16)


def outer_weight(w_ref, block):
    block[...] = jnp.zeros_like(block)
    for c in range(32):
        one = w_ref[c * 32 : c * 32 + 32, :]
        for j in range(4):
            block[c * 128 + j * 32 : c * 128 + j * 32 + 32, j * 128 : j * 128 + 128] = one


def outer_left(a, left_ref, left):
    for n in range(2):
        left[n, a] = left_ref[:, :, a, :, n * 128 : n * 128 + 128].reshape(512, 128).astype(F32)


def outer_right(a, right_ref, right):
    right[a] = right_ref[:, a].reshape(256, 256).T


def outer_products(las, ras, left, right, wide):
    count = 16 * len(las)
    for first in range(0, 32, 8):
        rows = jnp.concatenate(
            [
                jnp.concatenate([left[n, a, pl.ds(c, 16, stride=32), :] for n in range(2)], axis=1)
                for c in range(first, first + 8)
                for a in las
            ],
            axis=0,
        ).astype(BF16)
        for ra in ras:
            product = (dot(rows, right[ra]) * (1.0 / 256)).astype(BF16)
            for c in range(8):
                for half in range(2):
                    at = (first + c) * 128
                    wide[ra * 2 + half, las[0] * 16 : las[0] * 16 + count, at : at + 128] = product[
                        c * count : c * count + count, half * 128 : half * 128 + 128
                    ]


def outer_update(groups, las, wide, block, pairs):
    parts = []
    for (low, high), some in zip(groups, las):
        count = 16 * len(some)
        parts.append(wide[low:high, some[0] * 16 : some[0] * 16 + count, :].reshape((high - low) * count, 4096))
    update = dot(jnp.concatenate(parts, axis=0), block[...])
    at = 0
    for (low, high), some in zip(groups, las):
        for g in range(low, high):
            for a in some:
                for o in range(4):
                    pairs[pl.ds(a * 32 + (g % 2) * 16 + o * 4 + g // 2, 16, stride=128), :] = update[
                        at : at + 16, o * 128 : o * 128 + 128
                    ]
                at += 16


def whole_kernel(
    x_hbm, pair_hbm, bw_hbm, rw_hbm, ro_hbm, cw_hbm, co_hbm, ti_hbm, to_hbm, oi_hbm, oo_hbm,
    ao_hbm, pu_hbm,
    pair, bw, rw, ro, cw, co, ti, to, oi, oo,
    own, xo, bias, qd, kk, vt, gt, mask, mid, mix, wt, sendbuf, cells, fl, fr, lo, ri, left, right, wide, block, pairs,
    ao, pu,
    nsend, nrecv, hrecv, srecv, lrecv, frecv, rrecv, lsem,
    hsend, ssend, xsend, xrecv, csend, crecv, lsend, fsend, rsend,
):
    s, r = lax.axis_index("seq"), lax.axis_index("res")
    here = s * RES + r
    pos = {"x": s // 2, "y": (s % 2) * 2 + r // 8, "z": (r % 8) // 2}
    core = r % 2
    sibling = (s, r + 1 - 2 * core)

    def near(dim, by):
        at = dict(pos)
        at[dim] = (pos[dim] + by) % 4
        return device(at["x"], at["y"], at["z"], core)

    loads = {}
    for k, (name, src, dst) in enumerate(
        (
            ("pair", pair_hbm, pair), ("bw", bw_hbm, bw), ("rw", rw_hbm, rw), ("ro", ro_hbm, ro), ("cw", cw_hbm, cw),
            ("co", co_hbm, co), ("ti", ti_hbm, ti), ("to", to_hbm, to), ("oi", oi_hbm, oi), ("oo", oo_hbm, oo),
            ("keep", x_hbm.at[r], xo.at[r]),
        )
    ):
        loads[name] = pltpu.make_async_copy(src, dst, lsem.at[k])
        loads[name].start()

    def need(name):
        loads.pop(name).wait()

    barrier = pltpu.get_barrier_semaphore()

    def greet(k, carry):
        pl.semaphore_signal(barrier, inc=1, device_id=(s, (r + k) % 16), device_id_type=MESH)
        return carry

    lax.fori_loop(1, 16, greet, 0)
    for dim in "xy":
        for by in (1, 2, 3):
            pl.semaphore_signal(barrier, inc=1, device_id=near(dim, by), device_id_type=MESH)

    need("pair")
    need("bw")
    pair_bias(pair, bw, own)
    mine_at = bias.at[:, 0, pos["y"], pos["z"], core]
    bias[:, 0, pos["y"], pos["z"], core] = own[...]
    pl.semaphore_wait(barrier, 21)

    def scatter_x(k, carry):
        other = (r + k) % 16
        remote(x_hbm.at[other], xo.at[r], xsend, xrecv, (s, other)).start()
        return carry

    px, py, pz = pos["x"], pos["y"], pos["z"]
    ALL, MOST, REST = pl.ds(0, 4), pl.ds(0, 3), pl.ds(1, 3)
    LOW, HIGH = pl.ds(0, 2), pl.ds(2, 2)
    HALVES = (LOW, HIGH)
    BY = (1, 3, 2)
    PARTS = [(kind, by) for by in (0, 3, 1, 2) for kind in "yz"]

    def part_of(dx, k, inner=ALL):
        kind, by = PARTS[k]
        if kind == "y":
            return bias.at[LOW, dx, (py + by) % 4, inner, core]
        return bias.at[2, dx, inner, (pz + by) % 4, core]

    def share(group, what):
        remote(what, what, ssend, srecv.at[group], sibling).start()

    def along_x(k):
        for way, by in enumerate((1, 3)):
            remote(part_of(0, k), part_of(4 - by, k), hsend, hrecv.at[k, way], near("x", by)).start()

    def onward_x(*ks):
        for k in ks:
            for way, by in enumerate((1, 3)):
                got = part_of(4 - by, k)
                remote(got, got, hsend, hrecv.at[k, way], near("x", by)).wait_recv()
                remote(
                    part_of(4 - by, k, HALVES[way]), part_of(2, k, HALVES[way]), hsend, hrecv.at[k, 2 + way], near("x", by)
                ).start()
                share(4 - by, got)

    def last_x(*ks):
        for k in ks:
            for way, by in enumerate((1, 3)):
                half = part_of(2, k, HALVES[way])
                remote(half, half, hsend, hrecv.at[k, 2 + way], near("x", by)).wait_recv()
            share(2, part_of(2, k))

    def shared(group):
        half = bias.at[ALL, 0, :, :, 1 - core] if group == 0 else bias.at[MOST, group, :, :, 1 - core]
        if group == 4:
            half = bias.at[3, REST, :, :, 1 - core]
        remote(half, half, hsend, srecv.at[group], sibling).wait_recv()

    copies = []

    def three(dim, src, dst, base):
        made = [remote(src, dst, nsend.at[base + k], nrecv.at[base + k], near(dim, by)) for k, by in enumerate(BY)]
        for copy in made:
            copy.start()
        copies.extend(made)
        return made

    def arrived(made):
        for copy in made:
            copy.wait_recv()

    low_z = three("z", own.at[LOW], bias.at[LOW, 0, py, pz, core], 0)
    high_y = three("y", own.at[HIGH], bias.at[HIGH, 0, py, pz, core], 3)
    t_x = []
    for k, by in enumerate(BY):
        t_x.append(remote(own.at[3], bias.at[3, 4 - by, py, pz, core], nsend.at[6 + k], nrecv.at[6 + k], near("x", by)))
        t_x[k].start()
    copies.extend(t_x)
    lax.fori_loop(1, 16, scatter_x, 0)

    arrived(low_z)
    mine = bias.at[LOW, 0, py, :, core]
    low_y = three("y", mine, mine, 9)
    along_x(0)
    arrived(high_y)
    mine = bias.at[HIGH, 0, :, pz, core]
    high_z = three("z", mine, mine, 12)
    along_x(1)
    arrived(t_x)
    mine = bias.at[3, REST, py, pz, core]
    t_y = three("y", mine, mine, 15)
    row = lax.broadcasted_iota(jnp.int32, (C, 512), 0) // D
    lane = lax.broadcasted_iota(jnp.int32, (C, 512), 1) // 64
    mask[...] = jnp.where(row == lane, 1.0, 0.0).astype(BF16)
    need("rw")
    for i, at in enumerate((0, 2, 3)):
        wt[0, i * C : i * C + C, :] = rw[:, at * C : at * C + C].T
    for k in range(3):
        low_y[k].wait_recv()
        along_x(2 + 2 * k)
        high_z[k].wait_recv()
        along_x(3 + 2 * k)
        if k == 0:
            onward_x(0, 1)
    share(0, bias.at[:, 0, :, :, core])
    arrived(t_y)
    mine = bias.at[3, REST, :, pz, core]
    t_z = three("z", mine, mine, 18)
    need("keep")
    most = xo.at[pl.ds(0, 15)]
    remote(most, most, xsend, xrecv, sibling).wait()
    row_project(0, xo, wt.at[0], rw[:, C : 2 * C], qd, kk, vt, gt)
    onward_x(2, 3)
    row_project(1, xo, wt.at[0], rw[:, C : 2 * C], qd, kk, vt, gt)
    onward_x(4, 5)
    need("oo")
    outer_weight(oo, block)
    need("cw")
    for i, at in enumerate((0, 2, 3)):
        wt[1, i * C : i * C + C, :] = cw[:, at * C : at * C + C].T
    arrived(t_z)
    share(4, bias.at[3, REST, :, :, core])
    need("ro")

    def attend(q, carry):
        dx = q - q // 2 + 2 * (q % 2) * (1 - q // 2)
        sp = (px + dx) % 4

        @pl.when(q == 0)
        def _():
            shared(0)

        @pl.when(q == 1)
        def _():
            onward_x(6, 7)
            last_x(0, 1)
            shared(4)
            shared(3)

        @pl.when(q == 2)
        def _():
            last_x(2, 3, 4, 5)
            shared(1)

        @pl.when(q == 3)
        def _():
            last_x(6, 7)
            shared(2)

        row_attend(sp, dx, xo, bias, ro, qd, kk, vt, gt, mask, mid, mix)
        rows = mix[pl.ds(pl.multiple_of(sp * 512, 512), 512), :].astype(BF16)
        sendbuf[pl.ds(sp * 32, 32)] = rows.reshape(32, 16, 128)

        for yh in range(2):
            to_s = sp * 2 + yh

            def scatter(i, carry):
                to_r = lax.bitwise_and(r + i, 15)
                other = to_s * 16 + to_r

                @pl.when(other != here)
                def _():
                    remote(sendbuf.at[other], cells.at[here], csend, crecv, (to_s, to_r)).start()

                return carry

            lax.fori_loop(0, 16, scatter, 0, unroll=True)
        return carry

    lax.fori_loop(0, 4, attend, 0, unroll=True)
    cells[here] = sendbuf[here]
    for copy in copies:
        copy.wait_send()
    most = bias.at[:, :, :, :, 0]
    remote(most, most, ssend, srecv.at[0], sibling).wait_send()
    most = bias.at[MOST, MOST, :, :, 0]
    remote(most, most, hsend, srecv.at[0], sibling).wait_send()
    for name in ("co", "ti", "to", "oi"):
        need(name)
    most = cells.at[pl.ds(0, 127)]
    remote(most, most, csend, crecv, sibling).wait()

    mix[...] = cells[...].reshape(2048, 128).astype(F32)
    wf = oi[...]
    column = 2 * s + r // 8
    is_own = column == r
    chip = r // 2

    def onward_left(a):
        most = lo.at[pl.ds(0, 7), core, a]
        remote(most, most, lsend, lrecv.at[a], sibling).wait_recv()
        line = lo.at[:, core, a]
        remote(line, line, fsend, frecv.at[a], sibling).start()

    def residue(a, carry):
        factor = column_step(a, mix, wt.at[1], cw[:, C : 2 * C], co, ti, to, wf)
        fl[a] = factor[:D]
        fr[a] = factor[D:]
        lo[chip, core, a] = factor[:D]

        @pl.when(is_own)
        def _():
            ri[r % 8, a] = factor[D:]

        def send_left(k, carry):
            remote(fl.at[a], lo.at[chip, core, a], lsend, lrecv.at[a], (s, lax.bitwise_and(chip + k, 7) * 2 + core)).start()
            return carry

        def send_right(k, carry):
            @pl.when(jnp.logical_not(jnp.logical_and(is_own, k == 0)))
            def _():
                remote(fr.at[a], ri.at[r % 8, a], rsend, rrecv.at[a], (lax.bitwise_and(s + k, 7), column)).start()

            return carry

        lax.fori_loop(1, 8, send_left, 0, unroll=True)
        lax.fori_loop(0, 8, send_right, 0, unroll=True)

        @pl.when(a > 0)
        def _():
            onward_left(a - 1)

        return carry

    lax.fori_loop(0, 4, residue, 0)
    new = mix[...].astype(BF16).reshape(256, 8, 128)
    for ch in range(2):
        ao[:, :, ch * 128 : ch * 128 + 128] = new[:, ch * 4 : ch * 4 + 4, :]
    save = pltpu.make_async_copy(ao, ao_hbm, lsem.at[0])
    save.start()

    def gathered(a):
        half = lo.at[:, 1 - core, a]
        remote(half, half, fsend, frecv.at[a], sibling).wait_recv()

        @pl.when(is_own)
        def _():
            part = ri.at[pl.ds(0, 7), a]
            remote(part, part, rsend, rrecv.at[a], sibling).wait_recv()

        @pl.when(jnp.logical_not(is_own))
        def _():
            part = ri.at[:, a]
            remote(part, part, rsend, rrecv.at[a], sibling).wait_recv()

        outer_left(a, lo, left)
        outer_right(a, ri, right)

    for a in range(3):
        gathered(a)
    outer_products((0, 1, 2), (0, 1, 2), left, right, wide)
    onward_left(3)
    outer_update(((0, 6),), ((0, 1, 2),), wide, block, pairs)
    gathered(3)
    outer_products((3,), (0, 1, 2, 3), left, right, wide)
    outer_products((0, 1, 2), (3,), left, right, wide)
    outer_update(((0, 8), (6, 8)), ((3,), (0, 1, 2)), wide, block, pairs)
    pu[...] = pairs[...].astype(BF16)
    most = lo.at[pl.ds(0, 7), core]
    remote(most, most, lsend, lrecv.at[0], sibling).wait_send()
    half = lo.at[:, 1 - core]
    remote(half, half, fsend, lrecv.at[0], sibling).wait_send()

    @pl.when(is_own)
    def _():
        part = ri.at[pl.ds(0, 7)]
        remote(part, part, rsend, lrecv.at[0], sibling).wait_send()

    @pl.when(jnp.logical_not(is_own))
    def _():
        remote(ri, ri, rsend, lrecv.at[0], sibling).wait_send()

    last = pltpu.make_async_copy(pu, pu_hbm, lsem.at[1])
    last.start()
    last.wait()
    save.wait()


def body(
    alignment,
    pair_state,
    bias_weight,
    row_weight,
    row_output_weight,
    column_weight,
    column_output_weight,
    transition_in,
    transition_out,
    outer_in,
    outer_out,
):
    dma = pltpu.SemaphoreType.DMA
    new, update = pl.pallas_call(
        whole_kernel,
        out_shape=(jax.ShapeDtypeStruct((256, 4, C), BF16), jax.ShapeDtypeStruct((2048, 128), BF16)),
        in_specs=[ANY] * 11,
        out_specs=(ANY, ANY),
        scratch_shapes=[
            pltpu.VMEM((64, 32, 128), BF16),
            pltpu.VMEM((8, 128), BF16),
            pltpu.VMEM((C, 4 * C), BF16),
            pltpu.VMEM((C, C), BF16),
            pltpu.VMEM((C, 4 * C), BF16),
            pltpu.VMEM((C, C), BF16),
            pltpu.VMEM((C, 4 * C), BF16),
            pltpu.VMEM((4 * C, C), BF16),
            pltpu.VMEM((64, C), BF16),
            pltpu.VMEM((1024, 128), BF16),
            pltpu.VMEM((4, 32, 128), BF16),
            pltpu.VMEM((16, 2, 32, C), BF16),
            pltpu.VMEM((4, 4, 4, 4, 2, 32, 128), BF16),
            pltpu.VMEM((2, 8, C, 128), BF16),
            pltpu.VMEM((2, 512, C), BF16),
            pltpu.VMEM((2, C, 512), BF16),
            pltpu.VMEM((2, 4, C, 128), BF16),
            pltpu.VMEM((C, 512), BF16),
            pltpu.VMEM((2, 2, 128, 128), F32),
            pltpu.VMEM((2048, 128), F32),
            pltpu.VMEM((2, 3 * C, C), BF16),
            pltpu.VMEM((128, 16, 128), BF16),
            pltpu.VMEM((128, 16, 128), BF16),
            pltpu.VMEM((4, D, 256), BF16),
            pltpu.VMEM((4, D, 256), BF16),
            pltpu.VMEM((8, 2, 4, D, 256), BF16),
            pltpu.VMEM((8, 4, D, 256), BF16),
            pltpu.VMEM((2, 4, 512, 128), F32),
            pltpu.VMEM((4, 256, 256), BF16),
            pltpu.VMEM((8, 64, 4096), BF16),
            pltpu.VMEM((4096, 512), BF16),
            pltpu.VMEM((2048, 128), F32),
            pltpu.VMEM((256, 4, C), BF16),
            pltpu.VMEM((2048, 128), BF16),
            dma((21,)),
            dma((21,)),
            dma((8, 4)),
            dma((5,)),
            dma((4,)),
            dma((4,)),
            dma((4,)),
            dma((11,)),
        ]
        + [dma] * 9,
        compiler_params=pltpu.CompilerParams(collective_id=0, has_side_effects=True, vmem_limit_bytes=56 << 20),
        name="evoformer",
    )(
        alignment.reshape(16, 2, 32, C),
        pair_state,
        bias_weight.T,
        row_weight,
        row_output_weight,
        column_weight,
        column_output_weight,
        transition_in,
        transition_out,
        outer_in.T,
        outer_out,
    )
    pair_update = update.reshape(64, 32, 128)
    return (new, pair_update)


def solution(mesh):
    in_specs = (P("seq", "res", None), P("seq", "res", None)) + (P(),) * 9
    out_specs = (P(None, ("seq", "res"), None), P("seq", "res", None))
    return jax.shard_map(body, mesh=mesh, in_specs=in_specs, out_specs=out_specs, check_vma=False)
```
